32 devices in a mesh: dp: 32 (over z, y, x, core).
Axes of the slice: x: 2, y: 2, z: 4, core: 2. Of those that a mesh axis runs over, the one named last changes fastest.
Arguments:
- partials: bfloat16 [32, 256, 16384], P('dp'), may hold values from -24 to 24
- master: float32 [256, 16384], P('dp'), may hold values from -3 to 3
- moment_one: float32 [256, 16384], P('dp'), may hold values from -2 to 2
- moment_two: float32 [256, 16384], P('dp'), may hold values from 0.01 to 1
Outputs:
- master_new: float32 [256, 16384], P('dp')
- moment_one_new: float32 [256, 16384], P('dp')
- moment_two_new: float32 [256, 16384], P('dp')
- reduced_grad: float32 [256, 16384], P('dp')
- weights: bfloat16 [256, 16384], replicated
The draws below stay inside these ranges and needn't reach their ends.
All inputs are finite; a program needn't handle non-finite values. Where the reference program divides by a largest or mean magnitude, that divisor is 1e-20 or more.
Results may differ from the reference program's by a relative error of at most 0.012.
Values may be sent and summed in bfloat16 or wider, within the bound.
A program may use at most 128 MiB of HBM per device.

```python
import math
import jax
import jax.numpy as jnp
from jax import lax

W = 16384
BLOCK = 128
MBITS = 7
STEP = 20
ROWS = 256
N_DP = 32


def with_spikes(values, rng, source, target, parts, factor):
    owner, partner = [(jnp.arange(values.shape[dim]) // (values.shape[dim] // parts)).reshape([-1 if axis == dim else 1 for axis in range(values.ndim)]) for dim in (source, target)]
    chosen = jax.random.permutation(rng, parts)[partner]
    strong = (owner == chosen) | (owner == (partner + parts // 2) % parts)
    return jnp.where(strong, factor * values, values)


def levels(key, dims, split, smallest, high):
    loudness = 1.0
    for axis_at, shards_of in split:
        steps = jax.random.uniform(jax.random.fold_in(jax.random.fold_in(key, 6), axis_at), (shards_of,), jnp.float32, smallest / len(split), high / len(split))
        loudness = loudness * jnp.repeat(jnp.exp(steps), dims[axis_at] // shards_of).reshape((-1,) + (1,) * (len(dims) - 1 - axis_at))
    return loudness


def scatter_about(stream_key, shape, width, bound, split=(), dtype=jnp.bfloat16):
    level = levels(stream_key, shape, split, -0.22, 0.18) if split else 1.0
    array = jax.random.normal(stream_key, shape, jnp.float32) * width * level
    return jnp.minimum(jnp.maximum(array, -bound), bound).astype(dtype)


def noise_with(key, extent, width, most, pieces, heavy, dtype=jnp.bfloat16):
    values = width * jax.random.normal(key, extent, jnp.float32)
    if pieces:
        values = values * levels(key, extent, pieces, -0.22, 0.18)
    return jnp.clip(with_spikes(values, jax.random.fold_in(key, 3), *heavy), -most, most).astype(dtype)


def setup_inputs(seed: int = 0) -> dict:
    arg_keys = jax.random.split(jax.random.key(seed), 5)
    return {
        "partials": noise_with(arg_keys[0], (N_DP, ROWS, W), 4.0, 24.0, ((0, 32),), (0, 1, 32, 2.75)),
        "master": scatter_about(arg_keys[1], (ROWS, W), 0.5, 3.0, ((0, 32),), jnp.float32),
        "moment_one": scatter_about(arg_keys[2], (ROWS, W), 0.3, 2.0, ((0, 32),), jnp.float32),
        "moment_two": jnp.clip(jnp.exp(math.log(1.0) - 4.6051702 * jax.random.uniform(arg_keys[3], (ROWS, W), jnp.float32) ** levels(arg_keys[3], (ROWS, W), ((0, 32),), -0.2, 0.2)), 0.01, 1.0),
    }


def block_scale(amax):
    powers = jnp.asarray([2.0 ** k for k in range(-20, 13)], jnp.float32)
    doubled = jnp.asarray([2.0 ** (k + 1) for k in range(-20, 13)], jnp.float32)
    inverse = jnp.asarray([2.0 ** (MBITS - k - 1) for k in range(-20, 13)], jnp.float32)
    hit = amax[..., None] >= powers
    scale = lax.optimization_barrier(jnp.max(jnp.where(hit, doubled, jnp.float32(2.0 ** (-20))), axis=-1))
    mult = lax.optimization_barrier(jnp.min(jnp.where(hit, inverse, jnp.float32(2.0 ** (MBITS + 20))), axis=-1))
    return (scale, mult)

def reference(partials, master, moment_one, moment_two):
    nblk = W // BLOCK

    def max_step(carry, piece):
        mags = jnp.abs(piece.astype(jnp.float32)).reshape(ROWS, nblk, BLOCK)
        return (jnp.maximum(carry, lax.optimization_barrier(jnp.max(mags, axis=2))), None)
    amax, _ = lax.scan(max_step, jnp.zeros((ROWS, nblk), jnp.float32), partials)
    scale, mult = block_scale(amax)

    def sum_step(carry, piece):
        vals = piece.astype(jnp.float32).reshape(ROWS, nblk, BLOCK) * mult[:, :, None]
        mant = jnp.floor(vals + 0.5)
        return (carry + mant, None)
    total, _ = lax.scan(sum_step, jnp.zeros((ROWS, nblk, BLOCK), jnp.float32), partials)
    factor = scale / (2.0 ** MBITS * N_DP)
    reduced_grad = (total * factor[:, :, None]).reshape(ROWS, W)
    moment_one_new = 0.9 * moment_one + 0.1 * reduced_grad
    moment_two_new = 0.95 * moment_two + 0.05 * reduced_grad * reduced_grad
    first = moment_one_new / (1.0 - 0.9 ** STEP)
    second = moment_two_new / (1.0 - 0.95 ** STEP)
    update = first / (jnp.sqrt(second) + 1e-08)
    master_new = master - 0.001 * (update + 0.1 * master)
    blocks = master_new.reshape(ROWS, nblk, BLOCK)
    wscale = lax.optimization_barrier(jnp.max(jnp.abs(blocks), axis=2)) + 1e-06
    wmant = (blocks / wscale[:, :, None]).astype(jnp.bfloat16)
    weights = (wmant.astype(jnp.float32) * wscale[:, :, None]).reshape(ROWS, W).astype(jnp.bfloat16)
    return (master_new, moment_one_new, moment_two_new, reduced_grad, weights)
```

```python
import functools

import jax
import jax.numpy as jnp
from jax import lax
from jax.experimental import pallas as pl
from jax.experimental.pallas import tpu as pltpu
from jax.sharding import PartitionSpec as P

BLOCK = 128
MBITS = 7
STEP = 20
CHUNKS = 4
F32 = jnp.float32
BF16 = jnp.bfloat16


def adam(grad, master, one, two):
    one_new = 0.9 * one + 0.1 * grad
    two_new = 0.95 * two + 0.05 * grad * grad
    first = one_new / (1.0 - 0.9**STEP)
    second = two_new / (1.0 - 0.95**STEP)
    update = first / (jnp.sqrt(second) + 1e-08)
    return master - 0.001 * (update + 0.1 * master), one_new, two_new


def kernel(
    n,
    half,
    parts,
    master,
    one,
    two,
    master_new,
    one_new,
    two_new,
    grad_out,
    weights,
    own,
    peer,
    pair,
    amax,
    top_tx,
    top_rx,
    mult,
    factor,
    quad_rx,
    quad,
    duo_rx,
    duo,
    solo_rx,
    decoded,
    grad,
    w_tx,
    w_rows,
    gathered,
    load_sem,
    peer_send,
    peer_recv,
    top_send,
    top_recv,
    quad_send,
    quad_recv,
    duo_send,
    duo_recv,
    solo_send,
    solo_recv,
    grad_send,
    grad_recv,
    row_send,
    row_recv,
    g_send,
    g_recv,
    out_sem,
    out_send,
    out_recv,
):
    me = lax.axis_index("dp")
    core = me % 2
    x = (me // 2) % 2
    y = (me // 4) % 2
    z0 = (me // 8) % 2
    z1 = me // 16
    chip = me // 2
    other_core = me + 1 - 2 * core
    over_x = me + 2 * (1 - 2 * x)
    over_y = me + 4 * (1 - 2 * y)
    over_xy = over_x + 4 * (1 - 2 * y)
    over_z0 = me + 8 * (1 - 2 * z0)
    over_z1 = me + 16 * (1 - 2 * z1)
    over_z01 = over_z0 + 16 * (1 - 2 * z1)
    plane = (over_x, over_y, over_xy)
    line = (over_z0, over_z1, over_z01)
    width = half // CHUNKS
    nblk = width // BLOCK
    mine = core * half
    theirs = (1 - core) * half

    def remote(src, dst, send, recv, device):
        return pltpu.make_async_remote_copy(
            src_ref=src,
            dst_ref=dst,
            send_sem=send,
            recv_sem=recv,
            device_id=(device,),
            device_id_type=pl.DeviceIdType.MESH,
        )

    def at(start, size=width):
        return pl.ds(pl.multiple_of(start, BLOCK), size)

    loads = []
    for j in range(CHUNKS):
        c = pl.ds(j * width, width)
        loads.append(
            pltpu.make_async_copy(
                parts.at[:, :, :, :, :, at(mine + j * width)],
                own.at[:, :, :, :, :, c],
                load_sem.at[j],
            )
        )
        loads[j].start()

    barrier = pltpu.get_barrier_semaphore()
    for device in (other_core,) + plane + line:
        pl.semaphore_signal(
            barrier, inc=1, device_id=(device,), device_id_type=pl.DeviceIdType.MESH
        )
    pl.semaphore_wait(barrier, 7)

    swaps = []
    for j in range(CHUNKS):
        c = pl.ds(j * width, width)
        swaps.append(
            remote(
                parts.at[:, :, :, :, :, at(theirs + j * width)],
                peer.at[:, :, :, :, :, c],
                peer_send.at[j],
                peer_recv.at[j],
                other_core,
            )
        )
        swaps[j].start()

    amax[...] = jnp.zeros_like(amax)
    lanes = lax.broadcasted_iota(jnp.int32, (BLOCK, BLOCK), 1)
    subs = lax.broadcasted_iota(jnp.int32, (BLOCK, BLOCK), 0)
    shift = half // BLOCK

    def block_max(b, _):
        c = at(b * BLOCK, BLOCK)
        for h in range(2):
            a = jnp.abs(own[h, :, :, :, :, c].reshape(BLOCK, BLOCK).astype(F32))
            p = jnp.abs(peer[h, :, :, :, :, c].reshape(BLOCK, BLOCK).astype(F32))
            m = jnp.max(jnp.maximum(a, p), axis=1, keepdims=True)
            amax[...] = jnp.where(lanes == b + h * shift, m, amax[...])
        return 0

    for j in range(CHUNKS):
        loads[j].wait()
        swaps[j].wait_recv()
        lax.fori_loop(j * nblk, (j + 1) * nblk, block_max, 0)

    for r, group in enumerate((plane, line)):
        top_tx[r] = amax[...].astype(BF16)
        copies = [
            remote(
                top_tx.at[r], top_rx.at[r, i], top_send.at[r, i], top_recv.at[r, i], device
            )
            for i, device in enumerate(group)
        ]
        for copy in copies:
            copy.start()
        for i, copy in enumerate(copies):
            copy.wait_recv()
        best = amax[...]
        for i in range(3):
            best = jnp.maximum(best, top_rx[r, i].astype(F32))
        amax[...] = best
        for copy in copies:
            copy.wait_send()

    top = amax[...]
    m = jnp.full((BLOCK, BLOCK), 2.0 ** (MBITS + 20), F32)
    f = jnp.full((BLOCK, BLOCK), 2.0**-20 / (2.0**MBITS * n), F32)
    for k in range(-20, 13):
        hit = top >= 2.0**k
        m = jnp.where(hit, 2.0 ** (MBITS - k - 1), m)
        f = jnp.where(hit, 2.0 ** (k + 1) / (2.0**MBITS * n), f)
    mult[...] = m.astype(BF16)
    factor[...] = f

    def spread(values, lane):
        pick = jnp.where(subs == lane, 1.0, 0.0).astype(BF16)
        return jnp.dot(values, pick, preferred_element_type=F32)

    def block_pair(b, _):
        c = at(b * BLOCK, BLOCK)
        for h in range(2):
            s = spread(mult[...], b + h * shift)
            a = own[h, :, :, :, :, c].reshape(BLOCK, BLOCK).astype(F32)
            p = peer[h, :, :, :, :, c].reshape(BLOCK, BLOCK).astype(F32)
            t = jnp.floor(a * s + 0.5) + jnp.floor(p * s + 0.5)
            pair[h, :, :, :, :, c] = t.astype(BF16).reshape(2, 2, 2, 16, BLOCK)
        return 0

    started = {}

    def start(j, key, copies):
        for copy in copies:
            copy.start()
        started[j, key] = copies

    def arrived(j, key):
        for copy in started[j, key]:
            copy.wait_recv()

    def cols(j):
        return pl.ds(j * width, width)

    def send_pair(j):
        lax.fori_loop(j * nblk, (j + 1) * nblk, block_pair, 0)
        c = cols(j)
        spots = ((y, 1 - x), (1 - y, x), (1 - y, 1 - x))
        start(
            j,
            "quad",
            [
                remote(
                    pair.at[:, :, yy, xx, :, c],
                    quad_rx.at[i, :, :, :, c],
                    quad_send.at[j, i],
                    quad_recv.at[j, i],
                    device,
                )
                for i, ((yy, xx), device) in enumerate(zip(spots, plane))
            ],
        )

    def send_quad(j):
        arrived(j, "quad")

        def body(b, _):
            c = at(b * BLOCK, BLOCK)
            t = pair[:, :, y, x, :, c].astype(F32)
            for i in range(3):
                t = t + quad_rx[i, :, :, :, c].astype(F32)
            quad[:, :, :, c] = t
            return 0

        lax.fori_loop(j * nblk, (j + 1) * nblk, body, 0)
        c = cols(j)
        start(
            j,
            "duo",
            [
                remote(
                    quad.at[:, 1 - z0, :, c],
                    duo_rx.at[:, :, c],
                    duo_send.at[j],
                    duo_recv.at[j],
                    over_z0,
                )
            ],
        )

    def send_duo(j):
        arrived(j, "duo")
        c = cols(j)
        duo[:, :, c] = quad[:, z0, :, c] + duo_rx[:, :, c]
        start(
            j,
            "solo",
            [
                remote(
                    duo.at[1 - z1, :, c],
                    solo_rx.at[:, c],
                    solo_send.at[j],
                    solo_recv.at[j],
                    over_z1,
                )
            ],
        )

    def send_grad(j):
        arrived(j, "solo")
        rows = pl.ds(pl.multiple_of((chip % 8) * 16, 16), 16)
        scales = factor[rows, :]

        def body(b, _):
            c = at(b * BLOCK, BLOCK)
            lane = b + (chip // 8) * shift
            near = jnp.where(lanes[:16] == lane, scales, 0.0)
            s = jnp.sum(near, axis=1, keepdims=True)
            t = (duo[z1, :, c] + solo_rx[:, c]) * s
            decoded[:, :, c] = t.reshape(2, 8, BLOCK)
            return 0

        lax.fori_loop(j * nblk, (j + 1) * nblk, body, 0, unroll=4)
        c = cols(j)
        grad[core, :, c] = decoded[core, :, c]
        start(
            j,
            "grad",
            [
                remote(
                    decoded.at[1 - core, :, c],
                    grad.at[core, :, c],
                    grad_send.at[j],
                    grad_recv.at[j],
                    other_core,
                )
            ],
        )

    def step(j, h):
        c = cols(j)
        far = at(h * half + j * width)
        g = grad[h, :, c]
        new, m1, m2 = adam(g, master[:, far], one[:, far], two[:, far])
        master_new[:, far] = new
        one_new[:, far] = m1
        two_new[:, far] = m2
        grad_out[:, far] = g
        blocks = []
        for i in range(nblk):
            v = new[:, i * BLOCK : (i + 1) * BLOCK]
            w = jnp.max(jnp.abs(v), axis=1, keepdims=True) + 1e-06
            blocks.append((v / w).astype(BF16).astype(F32) * w)
        return jnp.concatenate(blocks, axis=1)

    def send_rows(j):
        arrived(j, "grad")
        c = cols(j)
        w_tx[:, c] = step(j, 1 - core)
        start(
            j,
            "rows",
            [
                remote(
                    w_tx.at[:, c],
                    w_rows.at[core, :, c],
                    row_send.at[j],
                    row_recv.at[j],
                    other_core,
                )
            ],
        )
        w_rows[core, :, c] = step(j, core)

    def gather(j, key, i, spot, device):
        ref = gathered.at[spot]
        return remote(ref, ref, g_send.at[j, i], g_recv.at[j, i], device)

    def gather_z1(j):
        arrived(j, "rows")
        c = cols(j)
        gathered[z1, z0, y, x, :, c] = w_rows[:, :, c].reshape(16, width).astype(BF16)
        start(j, "g1", [gather(j, "g1", 0, (z1, z0, y, x, slice(None), c), over_z1)])

    def gather_z0(j):
        arrived(j, "g1")
        c = cols(j)
        start(j, "g2", [gather(j, "g2", 1, (slice(None), z0, y, x, slice(None), c), over_z0)])

    def streams(j):
        return (
            pl.ds(j * width, width // 2),
            pl.ds(j * width + width // 2, width // 2),
        )

    every = slice(None)

    def gather_first(j):
        arrived(j, "g2")
        ca, cb = streams(j)
        start(
            j,
            "g3",
            [
                gather(j, "g3", 2, (every, every, y, x, every, ca), over_y),
                gather(j, "g3", 3, (every, every, y, x, every, cb), over_x),
            ],
        )

    def gather_second(j):
        arrived(j, "g3")
        ca, cb = streams(j)
        start(
            j,
            "g4",
            [
                gather(j, "g4", 4, (every, every, every, x, every, ca), over_x),
                gather(j, "g4", 5, (every, every, y, every, every, cb), over_y),
            ],
        )

    local = {}

    def hand_out(j):
        arrived(j, "g4")
        c = cols(j)
        src = gathered.at[:, :, :, :, :, c]
        dst = weights.at[:, :, :, :, :, at(mine + j * width)]
        start(j, "out", [remote(src, dst, out_send.at[j], out_recv.at[j], other_core)])
        local[j] = pltpu.make_async_copy(src, dst, out_sem.at[j])
        local[j].start()

    stages = (
        send_pair,
        send_quad,
        send_duo,
        send_grad,
        send_rows,
        gather_z1,
        gather_z0,
        gather_first,
        gather_second,
        hand_out,
    )
    for t in range(CHUNKS + len(stages) - 1):
        for s in range(len(stages)):
            if 0 <= t - s < CHUNKS:
                stages[s](t - s)
    for j in range(CHUNKS):
        arrived(j, "out")
        local[j].wait()
        swaps[j].wait_send()
    for copies in started.values():
        for copy in copies:
            copy.wait_send()


def fused(partials, master, moment_one, moment_two):
    n = lax.axis_size("dp")
    rows, full = partials.shape[1:]
    half = full // 2
    dims = (2, 2, 2, 2, 16)
    vmem = pl.BlockSpec(memory_space=pltpu.VMEM)
    hbm = pl.BlockSpec(memory_space=pl.ANY)
    state = jax.ShapeDtypeStruct(master.shape, F32)
    dma = pltpu.SemaphoreType.DMA
    outs = pl.pallas_call(
        functools.partial(kernel, n, half),
        out_shape=(state,) * 4 + (jax.ShapeDtypeStruct(dims + (full,), BF16),),
        in_specs=[hbm, vmem, vmem, vmem],
        out_specs=(vmem,) * 4 + (hbm,),
        scratch_shapes=[
            pltpu.VMEM(dims + (half,), BF16),
            pltpu.VMEM(dims + (half,), BF16),
            pltpu.VMEM(dims + (half,), BF16),
            pltpu.VMEM((BLOCK, BLOCK), F32),
            pltpu.VMEM((2, BLOCK, BLOCK), BF16),
            pltpu.VMEM((2, 3, BLOCK, BLOCK), BF16),
            pltpu.VMEM((BLOCK, BLOCK), BF16),
            pltpu.VMEM((BLOCK, BLOCK), F32),
            pltpu.VMEM((3, 2, 2, 16, half), BF16),
            pltpu.VMEM((2, 2, 16, half), F32),
            pltpu.VMEM((2, 16, half), F32),
            pltpu.VMEM((2, 16, half), F32),
            pltpu.VMEM((16, half), F32),
            pltpu.VMEM((2, 8, half), F32),
            pltpu.VMEM((2, 8, half), F32),
            pltpu.VMEM((8, half), F32),
            pltpu.VMEM((2, 8, half), F32),
            pltpu.VMEM(dims + (half,), BF16),
            dma((CHUNKS,)),
            dma((CHUNKS,)),
            dma((CHUNKS,)),
            dma((2, 3)),
            dma((2, 3)),
            dma((CHUNKS, 3)),
            dma((CHUNKS, 3)),
            dma((CHUNKS,)),
            dma((CHUNKS,)),
            dma((CHUNKS,)),
            dma((CHUNKS,)),
            dma((CHUNKS,)),
            dma((CHUNKS,)),
            dma((CHUNKS,)),
            dma((CHUNKS,)),
            dma((CHUNKS, 6)),
            dma((CHUNKS, 6)),
            dma((CHUNKS,)),
            dma((CHUNKS,)),
            dma((CHUNKS,)),
        ],
        compiler_params=pltpu.CompilerParams(
            collective_id=0, has_side_effects=True, vmem_limit_bytes=56 * 2**20
        ),
        cost_estimate=pl.CostEstimate(
            flops=60 * rows * full, bytes_accessed=6 * rows * full, transcendentals=0
        ),
    )(partials.reshape(dims + (full,)), master, moment_one, moment_two)
    return outs[:4] + (outs[4].reshape(rows, full),)


def block_scale(amax):
    powers = jnp.asarray([2.0**k for k in range(-20, 13)], jnp.float32)
    doubled = jnp.asarray([2.0 ** (k + 1) for k in range(-20, 13)], jnp.float32)
    inverse = jnp.asarray([2.0 ** (MBITS - k - 1) for k in range(-20, 13)], jnp.float32)
    hit = amax[..., None] >= powers
    scale = jnp.max(jnp.where(hit, doubled, jnp.float32(2.0 ** (-20))), axis=-1)
    mult = jnp.min(jnp.where(hit, inverse, jnp.float32(2.0 ** (MBITS + 20))), axis=-1)
    return (scale, mult)


def per_device(partials, master, moment_one, moment_two):
    devices = lax.axis_size("dp")
    local = partials[0]
    rows = local.shape[0]
    width = local.shape[1]
    nblk = width // BLOCK
    owned = master.shape[0]
    mags = jnp.abs(local.astype(jnp.float32)).reshape(rows, nblk, BLOCK)
    shared = lax.pmax(jnp.max(mags, axis=2).astype(jnp.bfloat16), "dp").astype(jnp.float32)
    scale_all, mult = block_scale(shared)
    vals = local.astype(jnp.float32).reshape(rows, nblk, BLOCK) * mult[:, :, None]
    mant = jnp.floor(vals + 0.5).reshape(rows, width)
    total = lax.psum_scatter(mant, "dp", scatter_dimension=0, tiled=True)
    start = lax.axis_index("dp") * owned
    scale = lax.dynamic_slice_in_dim(scale_all, start, owned, 0)
    total = total.reshape(owned, nblk, BLOCK)
    factor = scale / (2.0**MBITS * devices)
    reduced_grad = (total * factor[:, :, None]).reshape(owned, width)
    moment_one_new = 0.9 * moment_one + 0.1 * reduced_grad
    moment_two_new = 0.95 * moment_two + 0.05 * reduced_grad * reduced_grad
    first = moment_one_new / (1.0 - 0.9**STEP)
    second = moment_two_new / (1.0 - 0.95**STEP)
    update = first / (jnp.sqrt(second) + 1e-08)
    master_new = master - 0.001 * (update + 0.1 * master)
    blocks = master_new.reshape(owned, nblk, BLOCK)
    wscale = jnp.max(jnp.abs(blocks), axis=2) + 1e-06
    wmant = (blocks / wscale[:, :, None]).astype(jnp.bfloat16)
    own_weights = (
        (wmant.astype(jnp.float32) * wscale[:, :, None]).reshape(owned, width).astype(jnp.bfloat16)
    )
    weights = lax.all_gather(own_weights, "dp", axis=0, tiled=True)
    return (master_new, moment_one_new, moment_two_new, reduced_grad, weights)


def step_on_device(partials, master, moment_one, moment_two):
    if lax.axis_size("dp") == 32 and master.shape[0] == 8 and partials.shape[2] == 128 * BLOCK:
        return fused(partials, master, moment_one, moment_two)
    return per_device(partials, master, moment_one, moment_two)


def solution(mesh):
    in_specs = (P("dp", None, None), P("dp", None), P("dp", None), P("dp", None))
    out_specs = (P("dp", None), P("dp", None), P("dp", None), P("dp", None), P())
    return jax.shard_map(
        step_on_device, mesh=mesh, in_specs=in_specs, out_specs=out_specs, check_vma=False
    )
```

```python
import functools

import jax
import jax.numpy as jnp
from jax import lax
from jax.experimental import pallas as pl
from jax.experimental.pallas import tpu as pltpu
from jax.sharding import PartitionSpec as P

BLOCK = 128
MBITS = 7
STEP = 20
CHUNKS = 8
SWAPS = 4
F32 = jnp.float32
BF16 = jnp.bfloat16


def adam(grad, master, one, two):
    one_new = 0.9 * one + 0.1 * grad
    two_new = 0.95 * two + 0.05 * grad * grad
    first = one_new / (1.0 - 0.9**STEP)
    second = two_new / (1.0 - 0.95**STEP)
    update = first / (jnp.sqrt(second) + 1e-08)
    return master - 0.001 * (update + 0.1 * master), one_new, two_new


def kernel(
    n,
    half,
    parts,
    master,
    one,
    two,
    results,
    weights,
    own,
    peer,
    pair,
    amax,
    top_tx,
    top_rx,
    mult,
    factor,
    quad_rx,
    quad,
    line_rx,
    state,
    fresh,
    gathered,
    load_sem,
    peer_send,
    peer_recv,
    state_sem,
    state_send,
    state_recv,
    top_send,
    top_recv,
    quad_send,
    quad_recv,
    line_send,
    line_recv,
    g_send,
    g_recv,
    out_sem,
    out_send,
    out_recv,
):
    me = lax.axis_index("dp")
    core = me % 2
    x = (me // 2) % 2
    y = (me // 4) % 2
    z0 = (me // 8) % 2
    z1 = me // 16
    chip = me // 2
    other_core = me + 1 - 2 * core
    over_x = me + 2 * (1 - 2 * x)
    over_y = me + 4 * (1 - 2 * y)
    over_xy = over_x + 4 * (1 - 2 * y)
    over_z0 = me + 8 * (1 - 2 * z0)
    over_z1 = me + 16 * (1 - 2 * z1)
    over_z01 = over_z0 + 16 * (1 - 2 * z1)
    plane = (over_x, over_y, over_xy)
    line = (over_z0, over_z1, over_z01)
    plane_spots = ((y, 1 - x), (1 - y, x), (1 - y, 1 - x))
    line_spots = ((z1, 1 - z0), (1 - z1, z0), (1 - z1, 1 - z0))
    width = half // CHUNKS
    nblk = width // BLOCK
    mine = core * half
    theirs = (1 - core) * half
    every = slice(None)

    def remote(src, dst, send, recv, device):
        return pltpu.make_async_remote_copy(
            src_ref=src,
            dst_ref=dst,
            send_sem=send,
            recv_sem=recv,
            device_id=(device,),
            device_id_type=pl.DeviceIdType.MESH,
        )

    def at(start, size=width):
        return pl.ds(pl.multiple_of(start, BLOCK), size)

    def cols(j):
        return pl.ds(j * width, width)

    loads = []
    for j in range(SWAPS):
        size = half // SWAPS
        loads.append(
            pltpu.make_async_copy(
                parts.at[:, :, :, :, :, at(mine + j * size, size)],
                own.at[:, :, :, :, :, pl.ds(j * size, size)],
                load_sem.at[j],
            )
        )
        loads[j].start()

    barrier = pltpu.get_barrier_semaphore()
    for device in (other_core,) + plane + line:
        pl.semaphore_signal(
            barrier, inc=1, device_id=(device,), device_id_type=pl.DeviceIdType.MESH
        )
    pl.semaphore_wait(barrier, 7)

    swaps = []
    for j in range(SWAPS):
        size = half // SWAPS
        swaps.append(
            remote(
                parts.at[:, :, :, :, :, at(theirs + j * size, size)],
                peer.at[:, :, :, :, :, pl.ds(j * size, size)],
                peer_send.at[j],
                peer_recv.at[j],
                other_core,
            )
        )
        swaps[j].start()
    states = []
    for i, ref in enumerate((master, one, two)):
        states.append(
            (
                pltpu.make_async_copy(ref.at[:, at(mine, half)], state.at[i, core], state_sem.at[i]),
                remote(
                    ref.at[:, at(theirs, half)],
                    state.at[i, core],
                    state_send.at[i],
                    state_recv.at[i],
                    other_core,
                ),
            )
        )
        for copy in states[i]:
            copy.start()

    amax[...] = jnp.zeros_like(amax)
    lanes = lax.broadcasted_iota(jnp.int32, (BLOCK, BLOCK), 1)
    subs = lax.broadcasted_iota(jnp.int32, (BLOCK, BLOCK), 0)
    shift = half // BLOCK

    def block_max(i, _):
        for h in range(2):
            best = amax[...]
            for u in range(4):
                b = i * 4 + u
                c = at(b * BLOCK, BLOCK)
                a = jnp.abs(own[h, :, :, :, :, c].reshape(BLOCK, BLOCK).astype(F32))
                p = jnp.abs(peer[h, :, :, :, :, c].reshape(BLOCK, BLOCK).astype(F32))
                m = jnp.max(jnp.maximum(a, p), axis=1, keepdims=True)
                best = jnp.where(lanes == b + h * shift, m, best)
            amax[...] = best
        return 0

    for j in range(SWAPS):
        loads[j].wait()
        swaps[j].wait_recv()
        steps = half // BLOCK // SWAPS // 4
        lax.fori_loop(j * steps, (j + 1) * steps, block_max, 0)

    for r, group in enumerate((plane, line)):
        top_tx[r] = amax[...].astype(BF16)
        copies = [
            remote(
                top_tx.at[r], top_rx.at[r, i], top_send.at[r, i], top_recv.at[r, i], device
            )
            for i, device in enumerate(group)
        ]
        for copy in copies:
            copy.start()
        for i, copy in enumerate(copies):
            copy.wait_recv()
        best = amax[...]
        for i in range(3):
            best = jnp.maximum(best, top_rx[r, i].astype(F32))
        amax[...] = best
        for copy in copies:
            copy.wait_send()

    top = amax[...]
    m = jnp.full((BLOCK, BLOCK), 2.0 ** (MBITS + 20), F32)
    f = jnp.full((BLOCK, BLOCK), 2.0**-20 / (2.0**MBITS * n), F32)
    for k in range(-20, 13):
        hit = top >= 2.0**k
        m = jnp.where(hit, 2.0 ** (MBITS - k - 1), m)
        f = jnp.where(hit, 2.0 ** (k + 1) / (2.0**MBITS * n), f)
    mult[...] = m.astype(BF16)
    factor[...] = f

    def spread(values, lane):
        pick = jnp.where(subs == lane, 1.0, 0.0).astype(BF16)
        return jnp.dot(values, pick, preferred_element_type=F32)

    def block_pair(b, _):
        c = at(b * BLOCK, BLOCK)
        for h in range(2):
            s = spread(mult[...], b + h * shift)
            a = own[h, :, :, :, :, c].reshape(BLOCK, BLOCK).astype(F32)
            p = peer[h, :, :, :, :, c].reshape(BLOCK, BLOCK).astype(F32)
            t = jnp.floor(a * s + 0.5) + jnp.floor(p * s + 0.5)
            pair[h, :, :, :, :, c] = t.astype(BF16).reshape(2, 2, 2, 16, BLOCK)
        return 0

    started = {}

    def start(j, key, copies):
        for copy in copies:
            copy.start()
        started[j, key] = copies

    def arrived(j, key):
        for copy in started[j, key]:
            copy.wait_recv()

    def send_pair(j):
        lax.fori_loop(j * nblk, (j + 1) * nblk, block_pair, 0, unroll=2)
        c = cols(j)
        start(
            j,
            "quad",
            [
                remote(
                    pair.at[:, :, yy, xx, :, c],
                    quad_rx.at[i, :, :, :, c],
                    quad_send.at[j, i],
                    quad_recv.at[j, i],
                    plane[i],
                )
                for i, (yy, xx) in enumerate(plane_spots)
            ],
        )

    def send_quad(j):
        arrived(j, "quad")

        def body(b, _):
            c = at(b * BLOCK, BLOCK)
            t = pair[:, :, y, x, :, c].astype(F32)
            for i in range(3):
                t = t + quad_rx[i, :, :, :, c].astype(F32)
            quad[:, :, :, c] = t
            return 0

        lax.fori_loop(j * nblk, (j + 1) * nblk, body, 0, unroll=2)
        c = cols(j)
        start(
            j,
            "line",
            [
                remote(
                    quad.at[a, b, :, c],
                    line_rx.at[i, :, c],
                    line_send.at[j, i],
                    line_recv.at[j, i],
                    line[i],
                )
                for i, (a, b) in enumerate(line_spots)
            ],
        )

    def gather(j, i, spot, device):
        ref = gathered.at[spot]
        return remote(ref, ref, g_send.at[j, i], g_recv.at[j, i], device)

    def update(j):
        if j == 0:
            for near, far in states:
                near.wait()
                far.wait_recv()
        arrived(j, "line")
        rows = pl.ds(pl.multiple_of((chip % 8) * 16, 16), 16)
        scales = factor[rows, :]

        def body(b, _):
            c = at(b * BLOCK, BLOCK)
            lane = b + (chip // 8) * shift
            near = jnp.where(lanes[:16] == lane, scales, 0.0)
            s = jnp.sum(near, axis=1, keepdims=True)
            t = quad[z1, z0, :, c]
            for i in range(3):
                t = t + line_rx[i, :, c]
            g = (t * s).reshape(2, 8, BLOCK)
            new, m1, m2 = adam(g, state[0, :, :, c], state[1, :, :, c], state[2, :, :, c])
            fresh[0, :, :, c] = new
            fresh[1, :, :, c] = m1
            fresh[2, :, :, c] = m2
            fresh[3, :, :, c] = g
            v = new.reshape(16, BLOCK)
            w = jnp.max(jnp.abs(v), axis=1, keepdims=True) + 1e-06
            v = (v / w).astype(BF16).astype(F32) * w
            gathered[z1, z0, y, x, :, c] = v.astype(BF16)
            return 0

        lax.fori_loop(j * nblk, (j + 1) * nblk, body, 0, unroll=4)
        c = cols(j)
        spot = (z1, z0, y, x, every, c)
        start(j, "g1", [gather(j, i, spot, device) for i, device in enumerate(line)])
        c_out = at(mine + j * width)
        start(
            j,
            "state",
            [
                remote(
                    fresh.at[:, 1 - core, :, c],
                    results.at[:, :, c_out],
                    out_send.at[j, 0],
                    out_recv.at[j, 0],
                    other_core,
                )
            ],
        )
        keep(fresh.at[:, core, :, c], results.at[:, :, c_out], out_sem.at[j, 0])

    kept = []

    def keep(src, dst, sem):
        kept.append(pltpu.make_async_copy(src, dst, sem))
        kept[-1].start()

    def gather_first(j):
        arrived(j, "g1")
        ca = pl.ds(j * width, width // 2)
        cb = pl.ds(j * width + width // 2, width // 2)
        start(
            j,
            "g2",
            [
                gather(j, 3, (every, every, y, x, every, ca), over_y),
                gather(j, 4, (every, every, y, x, every, cb), over_x),
            ],
        )

    def gather_second(j):
        arrived(j, "g2")
        ca = pl.ds(j * width, width // 2)
        cb = pl.ds(j * width + width // 2, width // 2)
        start(
            j,
            "g3",
            [
                gather(j, 5, (every, every, every, x, every, ca), over_x),
                gather(j, 6, (every, every, y, every, every, cb), over_y),
            ],
        )

    def hand_out(j):
        arrived(j, "g3")
        src = gathered.at[:, :, :, :, :, cols(j)]
        dst = weights.at[:, :, :, :, :, at(mine + j * width)]
        start(j, "out", [remote(src, dst, out_send.at[j, 1], out_recv.at[j, 1], other_core)])
        keep(src, dst, out_sem.at[j, 1])

    stages = (send_pair, send_quad, update, gather_first, gather_second, hand_out)
    for t in range(CHUNKS + len(stages) - 1):
        for s in range(len(stages)):
            if 0 <= t - s < CHUNKS:
                stages[s](t - s)
    for j in range(CHUNKS):
        arrived(j, "out")
        arrived(j, "state")
    for copy in kept:
        copy.wait()
    for swap in swaps:
        swap.wait_send()
    for _, far in states:
        far.wait_send()
    for copies in started.values():
        for copy in copies:
            copy.wait_send()


def hand_over(results, weights, master_new, one_new, two_new, grad, out, sem):
    copies = [
        pltpu.make_async_copy(results.at[i], ref, sem.at[16 + i])
        for i, ref in enumerate((master_new, one_new, two_new, grad))
    ]
    for i in range(16):
        spot = (i // 8, i // 4 % 2, i // 2 % 2, i % 2)
        copies.append(pltpu.make_async_copy(weights.at[spot], out.at[spot], sem.at[i]))
    for copy in copies:
        copy.start()
    for copy in copies:
        copy.wait()


def fused(partials, master, moment_one, moment_two):
    n = lax.axis_size("dp")
    rows, full = partials.shape[1:]
    half = full // 2
    dims = (2, 2, 2, 2, 16)
    hbm = pl.BlockSpec(memory_space=pl.ANY)
    slab = jax.ShapeDtypeStruct(dims + (full,), BF16)
    dma = pltpu.SemaphoreType.DMA
    results, weights = pl.pallas_call(
        functools.partial(kernel, n, half),
        out_shape=(jax.ShapeDtypeStruct((4,) + master.shape, F32), slab),
        in_specs=[hbm] * 4,
        out_specs=(hbm, hbm),
        scratch_shapes=[
            pltpu.VMEM(dims + (half,), BF16),
            pltpu.VMEM(dims + (half,), BF16),
            pltpu.VMEM(dims + (half,), BF16),
            pltpu.VMEM((BLOCK, BLOCK), F32),
            pltpu.VMEM((2, BLOCK, BLOCK), BF16),
            pltpu.VMEM((2, 3, BLOCK, BLOCK), BF16),
            pltpu.VMEM((BLOCK, BLOCK), BF16),
            pltpu.VMEM((BLOCK, BLOCK), F32),
            pltpu.VMEM((3, 2, 2, 16, half), BF16),
            pltpu.VMEM((2, 2, 16, half), F32),
            pltpu.VMEM((3, 16, half), F32),
            pltpu.VMEM((3, 2, 8, half), F32),
            pltpu.VMEM((4, 2, 8, half), F32),
            pltpu.VMEM(dims + (half,), BF16),
            dma((SWAPS,)),
            dma((SWAPS,)),
            dma((SWAPS,)),
            dma((3,)),
            dma((3,)),
            dma((3,)),
            dma((2, 3)),
            dma((2, 3)),
            dma((CHUNKS, 3)),
            dma((CHUNKS, 3)),
            dma((CHUNKS, 3)),
            dma((CHUNKS, 3)),
            dma((CHUNKS, 7)),
            dma((CHUNKS, 7)),
            dma((CHUNKS, 2)),
            dma((CHUNKS, 2)),
            dma((CHUNKS, 2)),
        ],
        compiler_params=pltpu.CompilerParams(
            collective_id=0, has_side_effects=True, vmem_limit_bytes=56 * 2**20
        ),
        cost_estimate=pl.CostEstimate(
            flops=60 * rows * full, bytes_accessed=6 * rows * full, transcendentals=0
        ),
    )(partials.reshape(dims + (full,)), master, moment_one, moment_two)
    outs = pl.pallas_call(
        hand_over,
        out_shape=(jax.ShapeDtypeStruct(master.shape, F32),) * 4 + (slab,),
        in_specs=[hbm] * 2,
        out_specs=(hbm,) * 5,
        scratch_shapes=[dma((20,))],
        cost_estimate=pl.CostEstimate(
            flops=0, bytes_accessed=5 * rows * full, transcendentals=0
        ),
    )(results, weights)
    return outs[:4] + (outs[4].reshape(rows, full),)


def block_scale(amax):
    powers = jnp.asarray([2.0**k for k in range(-20, 13)], jnp.float32)
    doubled = jnp.asarray([2.0 ** (k + 1) for k in range(-20, 13)], jnp.float32)
    inverse = jnp.asarray([2.0 ** (MBITS - k - 1) for k in range(-20, 13)], jnp.float32)
    hit = amax[..., None] >= powers
    scale = jnp.max(jnp.where(hit, doubled, jnp.float32(2.0 ** (-20))), axis=-1)
    mult = jnp.min(jnp.where(hit, inverse, jnp.float32(2.0 ** (MBITS + 20))), axis=-1)
    return (scale, mult)


def per_device(partials, master, moment_one, moment_two):
    devices = lax.axis_size("dp")
    local = partials[0]
    rows = local.shape[0]
    width = local.shape[1]
    nblk = width // BLOCK
    owned = master.shape[0]
    mags = jnp.abs(local.astype(jnp.float32)).reshape(rows, nblk, BLOCK)
    shared = lax.pmax(jnp.max(mags, axis=2).astype(jnp.bfloat16), "dp").astype(jnp.float32)
    scale_all, mult = block_scale(shared)
    vals = local.astype(jnp.float32).reshape(rows, nblk, BLOCK) * mult[:, :, None]
    mant = jnp.floor(vals + 0.5).reshape(rows, width)
    total = lax.psum_scatter(mant, "dp", scatter_dimension=0, tiled=True)
    start = lax.axis_index("dp") * owned
    scale = lax.dynamic_slice_in_dim(scale_all, start, owned, 0)
    total = total.reshape(owned, nblk, BLOCK)
    factor = scale / (2.0**MBITS * devices)
    reduced_grad = (total * factor[:, :, None]).reshape(owned, width)
    moment_one_new = 0.9 * moment_one + 0.1 * reduced_grad
    moment_two_new = 0.95 * moment_two + 0.05 * reduced_grad * reduced_grad
    first = moment_one_new / (1.0 - 0.9**STEP)
    second = moment_two_new / (1.0 - 0.95**STEP)
    update = first / (jnp.sqrt(second) + 1e-08)
    master_new = master - 0.001 * (update + 0.1 * master)
    blocks = master_new.reshape(owned, nblk, BLOCK)
    wscale = jnp.max(jnp.abs(blocks), axis=2) + 1e-06
    wmant = (blocks / wscale[:, :, None]).astype(jnp.bfloat16)
    own_weights = (
        (wmant.astype(jnp.float32) * wscale[:, :, None]).reshape(owned, width).astype(jnp.bfloat16)
    )
    weights = lax.all_gather(own_weights, "dp", axis=0, tiled=True)
    return (master_new, moment_one_new, moment_two_new, reduced_grad, weights)


def step_on_device(partials, master, moment_one, moment_two):
    if lax.axis_size("dp") == 32 and master.shape[0] == 8 and partials.shape[2] == 128 * BLOCK:
        return fused(partials, master, moment_one, moment_two)
    return per_device(partials, master, moment_one, moment_two)


def solution(mesh):
    in_specs = (P("dp", None, None), P("dp", None), P("dp", None), P("dp", None))
    out_specs = (P("dp", None), P("dp", None), P("dp", None), P("dp", None), P())
    return jax.shard_map(
        step_on_device, mesh=mesh, in_specs=in_specs, out_specs=out_specs, check_vma=False
    )
```

```python
import functools

import jax
import jax.numpy as jnp
from jax import lax
from jax.experimental import pallas as pl
from jax.experimental.pallas import tpu as pltpu
from jax.sharding import PartitionSpec as P

BLOCK = 128
MBITS = 7
STEP = 20
CHUNKS = 8
SWAPS = 4
F32 = jnp.float32
BF16 = jnp.bfloat16


def adam(grad, master, one, two):
    one_new = 0.9 * one + 0.1 * grad
    two_new = 0.95 * two + 0.05 * grad * grad
    first = one_new / (1.0 - 0.9**STEP)
    second = two_new / (1.0 - 0.95**STEP)
    update = first / (jnp.sqrt(second) + 1e-08)
    return master - 0.001 * (update + 0.1 * master), one_new, two_new


def encode(total):
    odd = total - 2.0 * jnp.floor(total * 0.5) > 0.5
    wide = jnp.where(odd, (total - 1.0) * 2.0**20, total * 2.0**10)
    return jnp.where(jnp.abs(total) <= 256.0, total, wide).astype(BF16)


def decode(code):
    size = jnp.abs(code)
    wide = jnp.where(size > 2.0**19, code * 2.0**-20 + 1.0, code * 2.0**-10)
    return jnp.where(size <= 256.0, code, wide)


def kernel(
    n,
    half,
    parts,
    master,
    one,
    two,
    results,
    weights,
    own,
    peer,
    pair,
    amax,
    top_tx,
    top_rx,
    mult,
    factor,
    half_rx,
    half_tx,
    quad_rx,
    quad,
    line_rx,
    state,
    fresh,
    gathered,
    load_sem,
    peer_send,
    peer_recv,
    state_sem,
    state_send,
    state_recv,
    top_send,
    top_recv,
    half_send,
    half_recv,
    quad_send,
    quad_recv,
    line_send,
    line_recv,
    g_send,
    g_recv,
    out_sem,
    out_send,
    out_recv,
):
    me = lax.axis_index("dp")
    core = me % 2
    x = (me // 2) % 2
    y = (me // 4) % 2
    z0 = (me // 8) % 2
    z1 = me // 16
    chip = me // 2
    other_core = me + 1 - 2 * core
    over_x = me + 2 * (1 - 2 * x)
    over_y = me + 4 * (1 - 2 * y)
    over_xy = over_x + 4 * (1 - 2 * y)
    over_z0 = me + 8 * (1 - 2 * z0)
    over_z1 = me + 16 * (1 - 2 * z1)
    over_z01 = over_z0 + 16 * (1 - 2 * z1)
    plane = (over_x, over_y, over_xy)
    line = (over_z0, over_z1, over_z01)
    line_spots = ((z1, 1 - z0), (1 - z1, z0), (1 - z1, 1 - z0))
    width = half // CHUNKS
    nblk = width // BLOCK
    mine = core * half
    theirs = (1 - core) * half
    every = slice(None)

    def remote(src, dst, send, recv, device):
        return pltpu.make_async_remote_copy(
            src_ref=src,
            dst_ref=dst,
            send_sem=send,
            recv_sem=recv,
            device_id=(device,),
            device_id_type=pl.DeviceIdType.MESH,
        )

    def at(start, size=width):
        return pl.ds(pl.multiple_of(start, BLOCK), size)

    def cols(j):
        return pl.ds(j * width, width)

    loads = []
    for j in range(SWAPS):
        size = half // SWAPS
        loads.append(
            pltpu.make_async_copy(
                parts.at[:, :, :, :, :, at(mine + j * size, size)],
                own.at[:, :, :, :, :, pl.ds(j * size, size)],
                load_sem.at[j],
            )
        )
        loads[j].start()

    barrier = pltpu.get_barrier_semaphore()
    for device in (other_core,) + plane + line:
        pl.semaphore_signal(
            barrier, inc=1, device_id=(device,), device_id_type=pl.DeviceIdType.MESH
        )
    pl.semaphore_wait(barrier, 7)

    swaps = []
    for j in range(SWAPS):
        size = half // SWAPS
        swaps.append(
            remote(
                parts.at[:, :, :, :, :, at(theirs + j * size, size)],
                peer.at[:, :, :, :, :, pl.ds(j * size, size)],
                peer_send.at[j],
                peer_recv.at[j],
                other_core,
            )
        )
        swaps[j].start()
    states = []
    for i, ref in enumerate((master, one, two)):
        states.append(
            (
                pltpu.make_async_copy(ref.at[:, at(mine, half)], state.at[i, core], state_sem.at[i]),
                remote(
                    ref.at[:, at(theirs, half)],
                    state.at[i, core],
                    state_send.at[i],
                    state_recv.at[i],
                    other_core,
                ),
            )
        )
        for copy in states[i]:
            copy.start()

    amax[...] = jnp.zeros_like(amax)
    lanes = lax.broadcasted_iota(jnp.int32, (BLOCK, BLOCK), 1)
    subs = lax.broadcasted_iota(jnp.int32, (BLOCK, BLOCK), 0)
    shift = half // BLOCK

    def block_max(g, i):
        for h in range(2):
            best = amax[g]
            for u in range(4):
                b = i * 4 + u
                c = at(b * BLOCK, BLOCK)
                a = jnp.abs(own[h, :, :, :, :, c].reshape(BLOCK, BLOCK).astype(F32))
                p = jnp.abs(peer[h, :, :, :, :, c].reshape(BLOCK, BLOCK).astype(F32))
                m = jnp.max(jnp.maximum(a, p), axis=1, keepdims=True)
                best = jnp.where(lanes == b + h * shift, m, best)
            amax[g] = best

    def find_max(j):
        loads[j].wait()
        swaps[j].wait_recv()
        steps = half // BLOCK // SWAPS // 4

        def body(i, _):
            block_max(min(j, 1), i)
            return 0

        lax.fori_loop(j * steps, (j + 1) * steps, body, 0)

    tops = {}

    def send_top(g, r):
        top_tx[g, r] = amax[g].astype(BF16)
        tops[g, r] = [
            remote(
                top_tx.at[g, r],
                top_rx.at[g, r, i],
                top_send.at[g, r, i],
                top_recv.at[g, r, i],
                device,
            )
            for i, device in enumerate((plane, line)[r])
        ]
        for copy in tops[g, r]:
            copy.start()

    def take_top(g, r):
        for copy in tops[g, r]:
            copy.wait_recv()
        best = amax[g]
        for i in range(3):
            best = jnp.maximum(best, top_rx[g, r, i].astype(F32))
        amax[g] = best

    def find_scales(g):
        top = amax[g]
        m = jnp.full((BLOCK, BLOCK), 2.0 ** (MBITS + 20), F32)
        f = jnp.full((BLOCK, BLOCK), 2.0**-20 / (2.0**MBITS * n), F32)
        for k in range(-20, 13):
            hit = top >= 2.0**k
            m = jnp.where(hit, 2.0 ** (MBITS - k - 1), m)
            f = jnp.where(hit, 2.0 ** (k + 1) / (2.0**MBITS * n), f)
        mult[g] = m.astype(BF16)
        factor[g] = f

    def spread(values, lane):
        pick = jnp.where(subs == lane, 1.0, 0.0).astype(BF16)
        return jnp.dot(values, pick, preferred_element_type=F32)

    def block_pair(g, b):
        c = at(b * BLOCK, BLOCK)
        for h in range(2):
            s = spread(mult[g], b + h * shift)
            a = own[h, :, :, :, :, c].reshape(BLOCK, BLOCK).astype(F32)
            p = peer[h, :, :, :, :, c].reshape(BLOCK, BLOCK).astype(F32)
            t = jnp.floor(a * s + 0.5) + jnp.floor(p * s + 0.5)
            pair[h, :, :, :, :, c] = t.astype(BF16).reshape(2, 2, 2, 16, BLOCK)

    early = CHUNKS // SWAPS

    def group(j):
        return 0 if j < early else 1

    started = {}

    def start(j, key, copies):
        for copy in copies:
            copy.start()
        started[j, key] = copies

    def arrived(j, key):
        for copy in started[j, key]:
            copy.wait_recv()

    def streams(j):
        return (
            pl.ds(j * width, width // 2),
            pl.ds(j * width + width // 2, width // 2),
        )

    def send_pair(j):
        def body(b, _):
            block_pair(group(j), b)
            return 0

        lax.fori_loop(j * nblk, (j + 1) * nblk, body, 0, unroll=2)
        ca, cb = streams(j)
        start(
            j,
            "half",
            [
                remote(
                    pair.at[:, :, :, 1 - x, :, ca],
                    half_rx.at[:, :, :, :, ca],
                    half_send.at[j, 0],
                    half_recv.at[j, 0],
                    over_x,
                ),
                remote(
                    pair.at[:, :, 1 - y, :, :, cb],
                    half_rx.at[:, :, :, :, cb],
                    half_send.at[j, 1],
                    half_recv.at[j, 1],
                    over_y,
                ),
            ],
        )

    def send_half(j):
        arrived(j, "half")

        def first(b, _):
            c = at(b * BLOCK, BLOCK)
            near = pair[:, :, y, x, :, c].astype(F32) + half_rx[:, :, y, :, c].astype(F32)
            far = pair[:, :, 1 - y, x, :, c].astype(F32) + half_rx[:, :, 1 - y, :, c].astype(F32)
            quad[:, :, :, c] = near
            half_tx[:, :, :, c] = encode(far)
            return 0

        def second(b, _):
            c = at(b * BLOCK, BLOCK)
            near = pair[:, :, y, x, :, c].astype(F32) + half_rx[:, :, x, :, c].astype(F32)
            far = pair[:, :, y, 1 - x, :, c].astype(F32) + half_rx[:, :, 1 - x, :, c].astype(F32)
            quad[:, :, :, c] = near
            half_tx[:, :, :, c] = encode(far)
            return 0

        middle = j * nblk + nblk // 2
        lax.fori_loop(j * nblk, middle, first, 0, unroll=2)
        lax.fori_loop(middle, (j + 1) * nblk, second, 0, unroll=2)
        start(
            j,
            "quad",
            [
                remote(
                    half_tx.at[:, :, :, c],
                    quad_rx.at[:, :, :, c],
                    quad_send.at[j, i],
                    quad_recv.at[j, i],
                    device,
                )
                for i, (c, device) in enumerate(zip(streams(j), (over_y, over_x)))
            ],
        )

    def send_quad(j):
        arrived(j, "quad")

        def body(b, _):
            c = at(b * BLOCK, BLOCK)
            quad[:, :, :, c] = quad[:, :, :, c] + decode(quad_rx[:, :, :, c].astype(F32))
            return 0

        lax.fori_loop(j * nblk, (j + 1) * nblk, body, 0, unroll=2)
        c = cols(j)
        start(
            j,
            "line",
            [
                remote(
                    quad.at[a, b, :, c],
                    line_rx.at[i, :, c],
                    line_send.at[j, i],
                    line_recv.at[j, i],
                    line[i],
                )
                for i, (a, b) in enumerate(line_spots)
            ],
        )

    def gather(j, i, spot, device):
        ref = gathered.at[spot]
        return remote(ref, ref, g_send.at[j, i], g_recv.at[j, i], device)

    def update(j):
        if j == 0:
            for near, far in states:
                near.wait()
                far.wait_recv()
        arrived(j, "line")
        rows = pl.ds(pl.multiple_of((chip % 8) * 16, 16), 16)
        scales = factor[group(j), rows, :]

        def body(b, _):
            c = at(b * BLOCK, BLOCK)
            lane = b + (chip // 8) * shift
            near = jnp.where(lanes[:16] == lane, scales, 0.0)
            s = jnp.sum(near, axis=1, keepdims=True)
            t = quad[z1, z0, :, c]
            for i in range(3):
                t = t + line_rx[i, :, c]
            g = (t * s).reshape(2, 8, BLOCK)
            new, m1, m2 = adam(g, state[0, :, :, c], state[1, :, :, c], state[2, :, :, c])
            fresh[0, :, :, c] = new
            fresh[1, :, :, c] = m1
            fresh[2, :, :, c] = m2
            fresh[3, :, :, c] = g
            v = new.reshape(16, BLOCK)
            w = jnp.max(jnp.abs(v), axis=1, keepdims=True) + 1e-06
            v = (v / w).astype(BF16).astype(F32) * w
            gathered[z1, z0, y, x, :, c] = v.astype(BF16)
            return 0

        lax.fori_loop(j * nblk, (j + 1) * nblk, body, 0, unroll=4)
        c = cols(j)
        spot = (z1, z0, y, x, every, c)
        start(j, "g1", [gather(j, i, spot, device) for i, device in enumerate(line)])
        c_out = at(mine + j * width)
        start(
            j,
            "state",
            [
                remote(
                    fresh.at[:, 1 - core, :, c],
                    results.at[:, :, c_out],
                    out_send.at[j, 0],
                    out_recv.at[j, 0],
                    other_core,
                )
            ],
        )
        keep(fresh.at[:, core, :, c], results.at[:, :, c_out], out_sem.at[j, 0])

    kept = []

    def keep(src, dst, sem):
        kept.append(pltpu.make_async_copy(src, dst, sem))
        kept[-1].start()

    def gather_first(j):
        arrived(j, "g1")
        ca, cb = streams(j)
        start(
            j,
            "g2",
            [
                gather(j, 3, (every, every, y, x, every, ca), over_y),
                gather(j, 4, (every, every, y, x, every, cb), over_x),
            ],
        )

    def gather_second(j):
        arrived(j, "g2")
        ca, cb = streams(j)
        start(
            j,
            "g3",
            [
                gather(j, 5, (every, every, every, x, every, ca), over_x),
                gather(j, 6, (every, every, y, every, every, cb), over_y),
            ],
        )

    def hand_out(j):
        arrived(j, "g3")
        src = gathered.at[:, :, :, :, :, cols(j)]
        dst = weights.at[:, :, :, :, :, at(mine + j * width)]
        start(j, "out", [remote(src, dst, out_send.at[j, 1], out_recv.at[j, 1], other_core)])
        keep(src, dst, out_sem.at[j, 1])

    find_max(0)
    send_top(0, 0)
    find_max(1)
    take_top(0, 0)
    send_top(0, 1)
    find_max(2)
    take_top(0, 1)
    find_scales(0)

    stages = (send_pair, send_half, send_quad, update, gather_first, gather_second, hand_out)
    for t in range(CHUNKS + len(stages) - 1):
        if t == early - 1:
            find_max(3)
            send_top(1, 0)
        if t == early:
            take_top(1, 1)
            find_scales(1)
        for s in range(len(stages)):
            if 0 <= t - s < CHUNKS:
                stages[s](t - s)
            if s == 0 and t == early - 1:
                take_top(1, 0)
                send_top(1, 1)
    for j in range(CHUNKS):
        arrived(j, "out")
        arrived(j, "state")
    for copy in kept:
        copy.wait()
    for swap in swaps:
        swap.wait_send()
    for copies in tops.values():
        for copy in copies:
            copy.wait_send()
    for _, far in states:
        far.wait_send()
    for copies in started.values():
        for copy in copies:
            copy.wait_send()


def hand_over(results, weights, master_new, one_new, two_new, grad, out, state, slab, sem_in, sem_out):
    copies = []
    for i, ref in enumerate((master_new, one_new, two_new, grad)):
        copies.append((results.at[i], state.at[i], ref))
    for i in range(16):
        spot = (i // 8, i // 4 % 2, i // 2 % 2, i % 2)
        copies.append((weights.at[spot], slab.at[spot], out.at[spot]))
    reads = [
        pltpu.make_async_copy(src, mid, sem_in.at[i]) for i, (src, mid, _) in enumerate(copies)
    ]
    writes = [
        pltpu.make_async_copy(mid, dst, sem_out.at[i]) for i, (_, mid, dst) in enumerate(copies)
    ]
    for read in reads:
        read.start()
    for read, write in zip(reads, writes):
        read.wait()
        write.start()
    for write in writes:
        write.wait()


def fused(partials, master, moment_one, moment_two):
    n = lax.axis_size("dp")
    rows, full = partials.shape[1:]
    half = full // 2
    dims = (2, 2, 2, 2, 16)
    hbm = pl.BlockSpec(memory_space=pl.ANY)
    slab = jax.ShapeDtypeStruct(dims + (full,), BF16)
    dma = pltpu.SemaphoreType.DMA
    results, weights = pl.pallas_call(
        functools.partial(kernel, n, half),
        out_shape=(jax.ShapeDtypeStruct((4,) + master.shape, F32), slab),
        in_specs=[hbm] * 4,
        out_specs=(hbm, hbm),
        scratch_shapes=[
            pltpu.VMEM(dims + (half,), BF16),
            pltpu.VMEM(dims + (half,), BF16),
            pltpu.VMEM(dims + (half,), BF16),
            pltpu.VMEM((2, BLOCK, BLOCK), F32),
            pltpu.VMEM((2, 2, BLOCK, BLOCK), BF16),
            pltpu.VMEM((2, 2, 3, BLOCK, BLOCK), BF16),
            pltpu.VMEM((2, BLOCK, BLOCK), BF16),
            pltpu.VMEM((2, BLOCK, BLOCK), F32),
            pltpu.VMEM((2, 2, 2, 16, half), BF16),
            pltpu.VMEM((2, 2, 16, half), BF16),
            pltpu.VMEM((2, 2, 16, half), BF16),
            pltpu.VMEM((2, 2, 16, half), F32),
            pltpu.VMEM((3, 16, half), F32),
            pltpu.VMEM((3, 2, 8, half), F32),
            pltpu.VMEM((4, 2, 8, half), F32),
            pltpu.VMEM(dims + (half,), BF16),
            dma((SWAPS,)),
            dma((SWAPS,)),
            dma((SWAPS,)),
            dma((3,)),
            dma((3,)),
            dma((3,)),
            dma((2, 2, 3)),
            dma((2, 2, 3)),
            dma((CHUNKS, 2)),
            dma((CHUNKS, 2)),
            dma((CHUNKS, 2)),
            dma((CHUNKS, 2)),
            dma((CHUNKS, 3)),
            dma((CHUNKS, 3)),
            dma((CHUNKS, 7)),
            dma((CHUNKS, 7)),
            dma((CHUNKS, 2)),
            dma((CHUNKS, 2)),
            dma((CHUNKS, 2)),
        ],
        compiler_params=pltpu.CompilerParams(
            collective_id=0, has_side_effects=True, vmem_limit_bytes=56 * 2**20
        ),
        cost_estimate=pl.CostEstimate(
            flops=60 * rows * full, bytes_accessed=6 * rows * full, transcendentals=0
        ),
    )(partials.reshape(dims + (full,)), master, moment_one, moment_two)
    outs = pl.pallas_call(
        hand_over,
        out_shape=(jax.ShapeDtypeStruct(master.shape, F32),) * 4 + (slab,),
        in_specs=[hbm] * 2,
        out_specs=(hbm,) * 5,
        scratch_shapes=[
            pltpu.VMEM((4,) + master.shape, F32),
            pltpu.VMEM(dims + (full,), BF16),
            dma((20,)),
            dma((20,)),
        ],
        compiler_params=pltpu.CompilerParams(vmem_limit_bytes=56 * 2**20),
        cost_estimate=pl.CostEstimate(
            flops=0, bytes_accessed=5 * rows * full, transcendentals=0
        ),
    )(results, weights)
    return outs[:4] + (outs[4].reshape(rows, full),)


def block_scale(amax):
    powers = jnp.asarray([2.0**k for k in range(-20, 13)], jnp.float32)
    doubled = jnp.asarray([2.0 ** (k + 1) for k in range(-20, 13)], jnp.float32)
    inverse = jnp.asarray([2.0 ** (MBITS - k - 1) for k in range(-20, 13)], jnp.float32)
    hit = amax[..., None] >= powers
    scale = jnp.max(jnp.where(hit, doubled, jnp.float32(2.0 ** (-20))), axis=-1)
    mult = jnp.min(jnp.where(hit, inverse, jnp.float32(2.0 ** (MBITS + 20))), axis=-1)
    return (scale, mult)


def per_device(partials, master, moment_one, moment_two):
    devices = lax.axis_size("dp")
    local = partials[0]
    rows = local.shape[0]
    width = local.shape[1]
    nblk = width // BLOCK
    owned = master.shape[0]
    mags = jnp.abs(local.astype(jnp.float32)).reshape(rows, nblk, BLOCK)
    shared = lax.pmax(jnp.max(mags, axis=2).astype(jnp.bfloat16), "dp").astype(jnp.float32)
    scale_all, mult = block_scale(shared)
    vals = local.astype(jnp.float32).reshape(rows, nblk, BLOCK) * mult[:, :, None]
    mant = jnp.floor(vals + 0.5).reshape(rows, width)
    total = lax.psum_scatter(mant, "dp", scatter_dimension=0, tiled=True)
    start = lax.axis_index("dp") * owned
    scale = lax.dynamic_slice_in_dim(scale_all, start, owned, 0)
    total = total.reshape(owned, nblk, BLOCK)
    factor = scale / (2.0**MBITS * devices)
    reduced_grad = (total * factor[:, :, None]).reshape(owned, width)
    moment_one_new = 0.9 * moment_one + 0.1 * reduced_grad
    moment_two_new = 0.95 * moment_two + 0.05 * reduced_grad * reduced_grad
    first = moment_one_new / (1.0 - 0.9**STEP)
    second = moment_two_new / (1.0 - 0.95**STEP)
    update = first / (jnp.sqrt(second) + 1e-08)
    master_new = master - 0.001 * (update + 0.1 * master)
    blocks = master_new.reshape(owned, nblk, BLOCK)
    wscale = jnp.max(jnp.abs(blocks), axis=2) + 1e-06
    wmant = (blocks / wscale[:, :, None]).astype(jnp.bfloat16)
    own_weights = (
        (wmant.astype(jnp.float32) * wscale[:, :, None]).reshape(owned, width).astype(jnp.bfloat16)
    )
    weights = lax.all_gather(own_weights, "dp", axis=0, tiled=True)
    return (master_new, moment_one_new, moment_two_new, reduced_grad, weights)


def step_on_device(partials, master, moment_one, moment_two):
    if lax.axis_size("dp") == 32 and master.shape[0] == 8 and partials.shape[2] == 128 * BLOCK:
        return fused(partials, master, moment_one, moment_two)
    return per_device(partials, master, moment_one, moment_two)


def solution(mesh):
    in_specs = (P("dp", None, None), P("dp", None), P("dp", None), P("dp", None))
    out_specs = (P("dp", None), P("dp", None), P("dp", None), P("dp", None), P())
    return jax.shard_map(
        step_on_device, mesh=mesh, in_specs=in_specs, out_specs=out_specs, check_vma=False
    )
```

```python
import functools

import jax
import jax.numpy as jnp
from jax import lax
from jax.experimental import pallas as pl
from jax.experimental.pallas import tpu as pltpu
from jax.sharding import PartitionSpec as P

BLOCK = 128
MBITS = 7
STEP = 20
WIDTHS = (8, 8, 12, 12, 8, 8, 4, 4)
CHUNKS = len(WIDTHS)
SWAPS = 4
F32 = jnp.float32
BF16 = jnp.bfloat16


def adam(grad, master, one, two):
    one_new = 0.9 * one + 0.1 * grad
    two_new = 0.95 * two + 0.05 * grad * grad
    first = one_new / (1.0 - 0.9**STEP)
    second = two_new / (1.0 - 0.95**STEP)
    update = first / (jnp.sqrt(second) + 1e-08)
    return master - 0.001 * (update + 0.1 * master), one_new, two_new


def encode(total, step):
    rest = total - step * jnp.floor(total * (1.0 / step))
    scale = jnp.full_like(total, 2.0**10)
    for r in range(1, step):
        scale = jnp.where(rest > r - 0.5, 2.0 ** (10 * r + 10), scale)
    return jnp.where(jnp.abs(total) <= 256.0, total, (total - rest) * scale).astype(BF16)


def decode(code, step):
    size = jnp.abs(code)
    total = code
    for r in range(step):
        total = jnp.where(size > 2.0 ** (10 * r + 14), code * 2.0 ** (-10 * r - 10) + r, total)
    return total


def kernel(
    n,
    half,
    parts,
    master,
    one,
    two,
    results,
    weights,
    own,
    peer,
    pair,
    amax,
    top_tx,
    top_rx,
    mult,
    factor,
    half_rx,
    half_tx,
    quad_rx,
    quad,
    line_tx,
    line_rx,
    state,
    fresh,
    gathered,
    load_sem,
    peer_send,
    peer_recv,
    state_sem,
    state_send,
    state_recv,
    top_send,
    top_recv,
    half_send,
    half_recv,
    quad_send,
    quad_recv,
    line_send,
    line_recv,
    g_send,
    g_recv,
    out_sem,
    out_send,
    out_recv,
):
    me = lax.axis_index("dp")
    core = me % 2
    x = (me // 2) % 2
    y = (me // 4) % 2
    z0 = (me // 8) % 2
    z1 = me // 16
    chip = me // 2
    other_core = me + 1 - 2 * core
    over_x = me + 2 * (1 - 2 * x)
    over_y = me + 4 * (1 - 2 * y)
    over_xy = over_x + 4 * (1 - 2 * y)
    over_z0 = me + 8 * (1 - 2 * z0)
    over_z1 = me + 16 * (1 - 2 * z1)
    over_z01 = over_z0 + 16 * (1 - 2 * z1)
    plane = (over_x, over_y, over_xy)
    line = (over_z0, over_z1, over_z01)
    line_spots = ((z1, 1 - z0), (1 - z1, z0), (1 - z1, 1 - z0))
    first_block = [sum(WIDTHS[:j]) for j in range(CHUNKS + 1)]
    mine = core * half
    theirs = (1 - core) * half
    every = slice(None)

    def remote(src, dst, send, recv, device):
        return pltpu.make_async_remote_copy(
            src_ref=src,
            dst_ref=dst,
            send_sem=send,
            recv_sem=recv,
            device_id=(device,),
            device_id_type=pl.DeviceIdType.MESH,
        )

    def at(start, size):
        return pl.ds(pl.multiple_of(start, BLOCK), size)

    def cols(j):
        return pl.ds(first_block[j] * BLOCK, WIDTHS[j] * BLOCK)

    def cols_out(j):
        return at(mine + first_block[j] * BLOCK, WIDTHS[j] * BLOCK)

    loads = []
    for j in range(SWAPS):
        size = half // SWAPS
        loads.append(
            pltpu.make_async_copy(
                parts.at[:, :, :, :, :, at(mine + j * size, size)],
                own.at[:, :, :, :, :, pl.ds(j * size, size)],
                load_sem.at[j],
            )
        )
        loads[j].start()

    barrier = pltpu.get_barrier_semaphore()
    for device in (other_core,) + plane + line:
        pl.semaphore_signal(
            barrier, inc=1, device_id=(device,), device_id_type=pl.DeviceIdType.MESH
        )
    pl.semaphore_wait(barrier, 7)

    swaps = []
    for j in range(SWAPS):
        size = half // SWAPS
        swaps.append(
            remote(
                parts.at[:, :, :, :, :, at(theirs + j * size, size)],
                peer.at[:, :, :, :, :, pl.ds(j * size, size)],
                peer_send.at[j],
                peer_recv.at[j],
                other_core,
            )
        )
        swaps[j].start()
    states = []
    for i, ref in enumerate((master, one, two)):
        states.append(
            (
                pltpu.make_async_copy(ref.at[:, at(mine, half)], state.at[i, core], state_sem.at[i]),
                remote(
                    ref.at[:, at(theirs, half)],
                    state.at[i, core],
                    state_send.at[i],
                    state_recv.at[i],
                    other_core,
                ),
            )
        )
        for copy in states[i]:
            copy.start()

    amax[...] = jnp.zeros_like(amax)
    lanes = lax.broadcasted_iota(jnp.int32, (BLOCK, BLOCK), 1)
    subs = lax.broadcasted_iota(jnp.int32, (BLOCK, BLOCK), 0)
    shift = half // BLOCK

    def block_max(g, i):
        for h in range(2):
            best = amax[g]
            for u in range(4):
                b = i * 4 + u
                c = at(b * BLOCK, BLOCK)
                a = jnp.abs(own[h, :, :, :, :, c].reshape(BLOCK, BLOCK))
                p = jnp.abs(peer[h, :, :, :, :, c].reshape(BLOCK, BLOCK))
                m = jnp.max(jnp.maximum(a, p).astype(F32), axis=1, keepdims=True)
                best = jnp.where(lanes == b + h * shift, m, best)
            amax[g] = best

    def find_max(j):
        loads[j].wait()
        swaps[j].wait_recv()
        steps = half // BLOCK // SWAPS // 4

        def body(i, _):
            block_max(min(j, 1), i)
            return 0

        lax.fori_loop(j * steps, (j + 1) * steps, body, 0)

    tops = {}

    def send_top(g, r):
        top_tx[g, r] = amax[g].astype(BF16)
        tops[g, r] = [
            remote(
                top_tx.at[g, r],
                top_rx.at[g, r, i],
                top_send.at[g, r, i],
                top_recv.at[g, r, i],
                device,
            )
            for i, device in enumerate((plane, line)[r])
        ]
        for copy in tops[g, r]:
            copy.start()

    def take_top(g, r):
        for copy in tops[g, r]:
            copy.wait_recv()
        best = amax[g]
        for i in range(3):
            best = jnp.maximum(best, top_rx[g, r, i].astype(F32))
        amax[g] = best

    def find_scales(g):
        top = amax[g]
        m = jnp.full((BLOCK, BLOCK), 2.0 ** (MBITS + 20), F32)
        f = jnp.full((BLOCK, BLOCK), 2.0**-20 / (2.0**MBITS * n), F32)
        for k in range(-20, 13):
            hit = top >= 2.0**k
            m = jnp.where(hit, 2.0 ** (MBITS - k - 1), m)
            f = jnp.where(hit, 2.0 ** (k + 1) / (2.0**MBITS * n), f)
        mult[g] = m.astype(BF16)
        factor[g] = f

    def spread(values, lane):
        pick = jnp.where(subs == lane, 1.0, 0.0).astype(BF16)
        return jnp.dot(values, pick, preferred_element_type=F32)

    def block_pair(g, b):
        c = at(b * BLOCK, BLOCK)
        for h in range(2):
            s = spread(mult[g], b + h * shift)
            a = own[h, :, :, :, :, c].reshape(BLOCK, BLOCK).astype(F32)
            p = peer[h, :, :, :, :, c].reshape(BLOCK, BLOCK).astype(F32)
            t = jnp.floor(a * s + 0.5) + jnp.floor(p * s + 0.5)
            pair[h, :, :, :, :, c] = t.astype(BF16).reshape(2, 2, 2, 16, BLOCK)

    early = 2

    def group(j):
        return 0 if j < early else 1

    started = {}

    def start(j, key, copies):
        for copy in copies:
            copy.start()
        started[j, key] = copies

    def arrived(j, key):
        for copy in started[j, key]:
            copy.wait_recv()

    def streams(j):
        size = WIDTHS[j] * BLOCK // 2
        start = first_block[j] * BLOCK
        return pl.ds(start, size), pl.ds(start + size, size)

    def send_pair(j):
        def body(b, _):
            block_pair(group(j), b)
            return 0

        lax.fori_loop(first_block[j], first_block[j + 1], body, 0, unroll=2)
        ca, cb = streams(j)
        start(
            j,
            "half",
            [
                remote(
                    pair.at[:, :, :, 1 - x, :, ca],
                    half_rx.at[:, :, :, :, ca],
                    half_send.at[j, 0],
                    half_recv.at[j, 0],
                    over_x,
                ),
                remote(
                    pair.at[:, :, 1 - y, :, :, cb],
                    half_rx.at[:, :, :, :, cb],
                    half_send.at[j, 1],
                    half_recv.at[j, 1],
                    over_y,
                ),
            ],
        )

    def send_half(j):
        arrived(j, "half")

        def first(b, _):
            c = at(b * BLOCK, BLOCK)
            near = pair[:, :, y, x, :, c].astype(F32) + half_rx[:, :, y, :, c].astype(F32)
            far = pair[:, :, 1 - y, x, :, c].astype(F32) + half_rx[:, :, 1 - y, :, c].astype(F32)
            quad[:, :, :, c] = near
            half_tx[:, :, :, c] = encode(far, 2)
            return 0

        def second(b, _):
            c = at(b * BLOCK, BLOCK)
            near = pair[:, :, y, x, :, c].astype(F32) + half_rx[:, :, x, :, c].astype(F32)
            far = pair[:, :, y, 1 - x, :, c].astype(F32) + half_rx[:, :, 1 - x, :, c].astype(F32)
            quad[:, :, :, c] = near
            half_tx[:, :, :, c] = encode(far, 2)
            return 0

        middle = first_block[j] + WIDTHS[j] // 2
        lax.fori_loop(first_block[j], middle, first, 0, unroll=2)
        lax.fori_loop(middle, first_block[j + 1], second, 0, unroll=2)
        start(
            j,
            "quad",
            [
                remote(
                    half_tx.at[:, :, :, c],
                    quad_rx.at[:, :, :, c],
                    quad_send.at[j, i],
                    quad_recv.at[j, i],
                    device,
                )
                for i, (c, device) in enumerate(zip(streams(j), (over_y, over_x)))
            ],
        )

    def send_quad(j):
        arrived(j, "quad")

        def body(b, _):
            c = at(b * BLOCK, BLOCK)
            total = quad[:, :, :, c] + decode(quad_rx[:, :, :, c].astype(F32), 2)
            quad[:, :, :, c] = total
            line_tx[:, :, :, c] = encode(total, 4)
            return 0

        lax.fori_loop(first_block[j], first_block[j + 1], body, 0, unroll=2)
        c = cols(j)
        start(
            j,
            "line",
            [
                remote(
                    line_tx.at[a, b, :, c],
                    line_rx.at[i, :, c],
                    line_send.at[j, i],
                    line_recv.at[j, i],
                    line[i],
                )
                for i, (a, b) in enumerate(line_spots)
            ],
        )

    def gather(j, i, spot, device):
        ref = gathered.at[spot]
        return remote(ref, ref, g_send.at[j, i], g_recv.at[j, i], device)

    def update(j):
        if j == 0:
            for near, far in states:
                near.wait()
                far.wait_recv()
        arrived(j, "line")
        rows = pl.ds(pl.multiple_of((chip % 8) * 16, 16), 16)
        scales = factor[group(j), rows, :]

        def body(b, _):
            c = at(b * BLOCK, BLOCK)
            lane = b + (chip // 8) * shift
            near = jnp.where(lanes[:16] == lane, scales, 0.0)
            s = jnp.sum(near, axis=1, keepdims=True)
            t = quad[z1, z0, :, c]
            for i in range(3):
                t = t + decode(line_rx[i, :, c].astype(F32), 4)
            g = (t * s).reshape(2, 8, BLOCK)
            new, m1, m2 = adam(g, state[0, :, :, c], state[1, :, :, c], state[2, :, :, c])
            fresh[0, :, :, c] = new
            fresh[1, :, :, c] = m1
            fresh[2, :, :, c] = m2
            fresh[3, :, :, c] = g
            v = new.reshape(16, BLOCK)
            w = jnp.max(jnp.abs(v), axis=1, keepdims=True) + 1e-06
            v = (v / w).astype(BF16).astype(F32) * w
            gathered[z1, z0, y, x, :, c] = v.astype(BF16)
            return 0

        lax.fori_loop(first_block[j], first_block[j + 1], body, 0, unroll=4)
        c = cols(j)
        c_out = cols_out(j)
        spot = (z1, z0, y, x, every, c)
        start(j, "g1", [gather(j, i, spot, device) for i, device in enumerate(line)])
        start(
            j,
            "state",
            [
                remote(
                    fresh.at[:, 1 - core, :, c],
                    results.at[:, :, c_out],
                    out_send.at[j, 0],
                    out_recv.at[j, 0],
                    other_core,
                )
            ],
        )
        keep(fresh.at[:, core, :, c], results.at[:, :, c_out], out_sem.at[j, 0])

    kept = []

    def keep(src, dst, sem):
        kept.append(pltpu.make_async_copy(src, dst, sem))
        kept[-1].start()

    def gather_first(j):
        arrived(j, "g1")
        ca, cb = streams(j)
        start(
            j,
            "g2",
            [
                gather(j, 3, (every, every, y, x, every, ca), over_y),
                gather(j, 4, (every, every, y, x, every, cb), over_x),
            ],
        )

    def gather_second(j):
        arrived(j, "g2")
        ca, cb = streams(j)
        start(
            j,
            "g3",
            [
                gather(j, 5, (every, every, every, x, every, ca), over_x),
                gather(j, 6, (every, every, y, every, every, cb), over_y),
            ],
        )

    def hand_out(j):
        arrived(j, "g3")
        src = gathered.at[:, :, :, :, :, cols(j)]
        dst = weights.at[:, :, :, :, :, cols_out(j)]
        start(j, "out", [remote(src, dst, out_send.at[j, 1], out_recv.at[j, 1], other_core)])
        keep(src, dst, out_sem.at[j, 1])

    find_max(0)
    send_top(0, 0)
    find_max(1)
    take_top(0, 0)
    send_top(0, 1)
    find_max(2)
    take_top(0, 1)
    find_scales(0)

    stages = (send_pair, send_half, send_quad, update, gather_first, gather_second, hand_out)
    for t in range(CHUNKS + len(stages) - 1):
        if t == early - 1:
            find_max(3)
            send_top(1, 0)
        if t == early:
            take_top(1, 1)
            find_scales(1)
        for s in range(len(stages)):
            if 0 <= t - s < CHUNKS:
                stages[s](t - s)
            if s == 0 and t == early - 1:
                take_top(1, 0)
                send_top(1, 1)
    for j in range(CHUNKS):
        arrived(j, "out")
        arrived(j, "state")
    for copy in kept:
        copy.wait()
    for swap in swaps:
        swap.wait_send()
    for copies in tops.values():
        for copy in copies:
            copy.wait_send()
    for _, far in states:
        far.wait_send()
    for copies in started.values():
        for copy in copies:
            copy.wait_send()


def hand_over(results, weights, master_new, one_new, two_new, grad, out, sem):
    copies = []
    for i in range(16):
        spot = (i // 8, i // 4 % 2, i // 2 % 2, i % 2)
        copies.append(pltpu.make_async_copy(weights.at[spot], out.at[spot], sem.at[i]))
    for i, ref in enumerate((master_new, one_new, two_new, grad)):
        copies.append(pltpu.make_async_copy(results.at[i], ref, sem.at[16 + i]))
    for copy in copies:
        copy.start()
    for copy in copies:
        copy.wait()


def fused(partials, master, moment_one, moment_two):
    n = lax.axis_size("dp")
    rows, full = partials.shape[1:]
    half = full // 2
    dims = (2, 2, 2, 2, 16)
    hbm = pl.BlockSpec(memory_space=pl.ANY)
    vmem = pl.BlockSpec(memory_space=pltpu.VMEM)
    slab = jax.ShapeDtypeStruct(dims + (full,), BF16)
    dma = pltpu.SemaphoreType.DMA
    results, weights = pl.pallas_call(
        functools.partial(kernel, n, half),
        out_shape=(pltpu.VMEM((4,) + master.shape, F32), pltpu.VMEM(dims + (full,), BF16)),
        in_specs=[hbm] * 4,
        out_specs=(hbm, hbm),
        scratch_shapes=[
            pltpu.VMEM(dims + (half,), BF16),
            pltpu.VMEM(dims + (half,), BF16),
            pltpu.VMEM(dims + (half,), BF16),
            pltpu.VMEM((2, BLOCK, BLOCK), F32),
            pltpu.VMEM((2, 2, BLOCK, BLOCK), BF16),
            pltpu.VMEM((2, 2, 3, BLOCK, BLOCK), BF16),
            pltpu.VMEM((2, BLOCK, BLOCK), BF16),
            pltpu.VMEM((2, BLOCK, BLOCK), F32),
            pltpu.VMEM((2, 2, 2, 16, half), BF16),
            pltpu.VMEM((2, 2, 16, half), BF16),
            pltpu.VMEM((2, 2, 16, half), BF16),
            pltpu.VMEM((2, 2, 16, half), F32),
            pltpu.VMEM((2, 2, 16, half), BF16),
            pltpu.VMEM((3, 16, half), BF16),
            pltpu.VMEM((3, 2, 8, half), F32),
            pltpu.VMEM((4, 2, 8, half), F32),
            pltpu.VMEM(dims + (half,), BF16),
            dma((SWAPS,)),
            dma((SWAPS,)),
            dma((SWAPS,)),
            dma((3,)),
            dma((3,)),
            dma((3,)),
            dma((2, 2, 3)),
            dma((2, 2, 3)),
            dma((CHUNKS, 2)),
            dma((CHUNKS, 2)),
            dma((CHUNKS, 2)),
            dma((CHUNKS, 2)),
            dma((CHUNKS, 3)),
            dma((CHUNKS, 3)),
            dma((CHUNKS, 7)),
            dma((CHUNKS, 7)),
            dma((CHUNKS, 2)),
            dma((CHUNKS, 2)),
            dma((CHUNKS, 2)),
        ],
        compiler_params=pltpu.CompilerParams(
            collective_id=0, has_side_effects=True, vmem_limit_bytes=52 * 2**20
        ),
        cost_estimate=pl.CostEstimate(
            flops=60 * rows * full, bytes_accessed=6 * rows * full, transcendentals=0
        ),
    )(partials.reshape(dims + (full,)), master, moment_one, moment_two)
    outs = pl.pallas_call(
        hand_over,
        out_shape=(jax.ShapeDtypeStruct(master.shape, F32),) * 4 + (slab,),
        in_specs=[vmem] * 2,
        out_specs=(hbm,) * 5,
        scratch_shapes=[
            dma((20,)),
        ],
        compiler_params=pltpu.CompilerParams(vmem_limit_bytes=8 * 2**20),
        cost_estimate=pl.CostEstimate(
            flops=0, bytes_accessed=5 * rows * full, transcendentals=0
        ),
    )(results, weights)
    return outs[:4] + (outs[4].reshape(rows, full),)


def block_scale(amax):
    powers = jnp.asarray([2.0**k for k in range(-20, 13)], jnp.float32)
    doubled = jnp.asarray([2.0 ** (k + 1) for k in range(-20, 13)], jnp.float32)
    inverse = jnp.asarray([2.0 ** (MBITS - k - 1) for k in range(-20, 13)], jnp.float32)
    hit = amax[..., None] >= powers
    scale = jnp.max(jnp.where(hit, doubled, jnp.float32(2.0 ** (-20))), axis=-1)
    mult = jnp.min(jnp.where(hit, inverse, jnp.float32(2.0 ** (MBITS + 20))), axis=-1)
    return (scale, mult)


def per_device(partials, master, moment_one, moment_two):
    devices = lax.axis_size("dp")
    local = partials[0]
    rows = local.shape[0]
    width = local.shape[1]
    nblk = width // BLOCK
    owned = master.shape[0]
    mags = jnp.abs(local.astype(jnp.float32)).reshape(rows, nblk, BLOCK)
    shared = lax.pmax(jnp.max(mags, axis=2).astype(jnp.bfloat16), "dp").astype(jnp.float32)
    scale_all, mult = block_scale(shared)
    vals = local.astype(jnp.float32).reshape(rows, nblk, BLOCK) * mult[:, :, None]
    mant = jnp.floor(vals + 0.5).reshape(rows, width)
    total = lax.psum_scatter(mant, "dp", scatter_dimension=0, tiled=True)
    start = lax.axis_index("dp") * owned
    scale = lax.dynamic_slice_in_dim(scale_all, start, owned, 0)
    total = total.reshape(owned, nblk, BLOCK)
    factor = scale / (2.0**MBITS * devices)
    reduced_grad = (total * factor[:, :, None]).reshape(owned, width)
    moment_one_new = 0.9 * moment_one + 0.1 * reduced_grad
    moment_two_new = 0.95 * moment_two + 0.05 * reduced_grad * reduced_grad
    first = moment_one_new / (1.0 - 0.9**STEP)
    second = moment_two_new / (1.0 - 0.95**STEP)
    update = first / (jnp.sqrt(second) + 1e-08)
    master_new = master - 0.001 * (update + 0.1 * master)
    blocks = master_new.reshape(owned, nblk, BLOCK)
    wscale = jnp.max(jnp.abs(blocks), axis=2) + 1e-06
    wmant = (blocks / wscale[:, :, None]).astype(jnp.bfloat16)
    own_weights = (
        (wmant.astype(jnp.float32) * wscale[:, :, None]).reshape(owned, width).astype(jnp.bfloat16)
    )
    weights = lax.all_gather(own_weights, "dp", axis=0, tiled=True)
    return (master_new, moment_one_new, moment_two_new, reduced_grad, weights)


def step_on_device(partials, master, moment_one, moment_two):
    if lax.axis_size("dp") == 32 and master.shape[0] == 8 and partials.shape[2] == 128 * BLOCK:
        return fused(partials, master, moment_one, moment_two)
    return per_device(partials, master, moment_one, moment_two)


def solution(mesh):
    in_specs = (P("dp", None, None), P("dp", None), P("dp", None), P("dp", None))
    out_specs = (P("dp", None), P("dp", None), P("dp", None), P("dp", None), P())
    return jax.shard_map(
        step_on_device, mesh=mesh, in_specs=in_specs, out_specs=out_specs, check_vma=False
    )
```

```python
import functools

import jax
import jax.numpy as jnp
from jax import lax
from jax.experimental import pallas as pl
from jax.experimental.pallas import tpu as pltpu
from jax.sharding import PartitionSpec as P

BLOCK = 128
MBITS = 7
STEP = 20
WIDTHS = (8, 8, 12, 12, 8, 8, 4, 4)
CHUNKS = len(WIDTHS)
LINE_LAST = (1, 4)
SWAPS = 4
F32 = jnp.float32
BF16 = jnp.bfloat16


def adam(grad, master, one, two):
    one_new = 0.9 * one + 0.1 * grad
    two_new = 0.95 * two + 0.05 * grad * grad
    first = one_new / (1.0 - 0.9**STEP)
    second = two_new / (1.0 - 0.95**STEP)
    update = first / (jnp.sqrt(second) + 1e-08)
    return master - 0.001 * (update + 0.1 * master), one_new, two_new


def encode(total, step):
    rest = total - step * jnp.floor(total * (1.0 / step))
    scale = jnp.full_like(total, 2.0**10)
    for r in range(1, step):
        scale = jnp.where(rest > r - 0.5, 2.0 ** (10 * r + 10), scale)
    return jnp.where(jnp.abs(total) <= 256.0, total, (total - rest) * scale).astype(BF16)


def decode(code, step):
    size = jnp.abs(code)
    total = code
    for r in range(step):
        total = jnp.where(size > 2.0 ** (10 * r + 14), code * 2.0 ** (-10 * r - 10) + r, total)
    return total


def kernel(
    n,
    half,
    parts,
    master,
    one,
    two,
    results,
    weights,
    own,
    peer,
    pair,
    amax,
    top_tx,
    top_rx,
    mult,
    factor,
    half_rx,
    half_tx,
    quad_rx,
    quad,
    line_tx,
    line_rx,
    state,
    fresh,
    gathered,
    load_sem,
    peer_send,
    peer_recv,
    state_sem,
    state_send,
    state_recv,
    top_send,
    top_recv,
    half_send,
    half_recv,
    quad_send,
    quad_recv,
    line_send,
    line_recv,
    g_send,
    g_recv,
    out_sem,
    out_send,
    out_recv,
):
    me = lax.axis_index("dp")
    core = me % 2
    x = (me // 2) % 2
    y = (me // 4) % 2
    z0 = (me // 8) % 2
    z1 = me // 16
    chip = me // 2
    other_core = me + 1 - 2 * core
    over_x = me + 2 * (1 - 2 * x)
    over_y = me + 4 * (1 - 2 * y)
    over_xy = over_x + 4 * (1 - 2 * y)
    over_z0 = me + 8 * (1 - 2 * z0)
    over_z1 = me + 16 * (1 - 2 * z1)
    over_z01 = over_z0 + 16 * (1 - 2 * z1)
    plane = (over_x, over_y, over_xy)
    line = (over_z0, over_z1, over_z01)
    line_spots = ((z1, 1 - z0), (1 - z1, z0), (1 - z1, 1 - z0))
    first_block = [sum(WIDTHS[:j]) for j in range(CHUNKS + 1)]
    mine = core * half
    theirs = (1 - core) * half
    every = slice(None)

    def remote(src, dst, send, recv, device):
        return pltpu.make_async_remote_copy(
            src_ref=src,
            dst_ref=dst,
            send_sem=send,
            recv_sem=recv,
            device_id=(device,),
            device_id_type=pl.DeviceIdType.MESH,
        )

    def at(start, size):
        return pl.ds(pl.multiple_of(start, BLOCK), size)

    def cols(j):
        return pl.ds(first_block[j] * BLOCK, WIDTHS[j] * BLOCK)

    def cols_out(j):
        return at(mine + first_block[j] * BLOCK, WIDTHS[j] * BLOCK)

    loads = []
    for j in range(SWAPS):
        size = half // SWAPS
        loads.append(
            pltpu.make_async_copy(
                parts.at[:, :, :, :, :, at(mine + j * size, size)],
                own.at[:, :, :, :, :, pl.ds(j * size, size)],
                load_sem.at[j],
            )
        )
        loads[j].start()

    barrier = pltpu.get_barrier_semaphore()
    for device in (other_core,) + plane + line:
        pl.semaphore_signal(
            barrier, inc=1, device_id=(device,), device_id_type=pl.DeviceIdType.MESH
        )
    pl.semaphore_wait(barrier, 7)

    swaps = []
    for j in range(SWAPS):
        size = half // SWAPS
        swaps.append(
            remote(
                parts.at[:, :, :, :, :, at(theirs + j * size, size)],
                peer.at[:, :, :, :, :, pl.ds(j * size, size)],
                peer_send.at[j],
                peer_recv.at[j],
                other_core,
            )
        )
        swaps[j].start()
    states = []
    for i, ref in enumerate((master, one, two)):
        states.append(
            (
                pltpu.make_async_copy(ref.at[:, at(mine, half)], state.at[i, core], state_sem.at[i]),
                remote(
                    ref.at[:, at(theirs, half)],
                    state.at[i, core],
                    state_send.at[i],
                    state_recv.at[i],
                    other_core,
                ),
            )
        )
        for copy in states[i]:
            copy.start()

    amax[...] = jnp.zeros_like(amax)
    lanes = lax.broadcasted_iota(jnp.int32, (BLOCK, BLOCK), 1)
    subs = lax.broadcasted_iota(jnp.int32, (BLOCK, BLOCK), 0)
    shift = half // BLOCK

    def block_max(g, i):
        for h in range(2):
            best = amax[g]
            for u in range(4):
                b = i * 4 + u
                c = at(b * BLOCK, BLOCK)
                a = jnp.abs(own[h, :, :, :, :, c].reshape(BLOCK, BLOCK))
                p = jnp.abs(peer[h, :, :, :, :, c].reshape(BLOCK, BLOCK))
                m = jnp.max(jnp.maximum(a, p).astype(F32), axis=1, keepdims=True)
                best = jnp.where(lanes == b + h * shift, m, best)
            amax[g] = best

    def find_max(j):
        loads[j].wait()
        swaps[j].wait_recv()
        steps = half // BLOCK // SWAPS // 4

        def body(i, _):
            block_max(min(j, 1), i)
            return 0

        lax.fori_loop(j * steps, (j + 1) * steps, body, 0)

    tops = {}

    def send_top(g, r):
        top_tx[g, r] = amax[g].astype(BF16)
        tops[g, r] = [
            remote(
                top_tx.at[g, r],
                top_rx.at[g, r, i],
                top_send.at[g, r, i],
                top_recv.at[g, r, i],
                device,
            )
            for i, device in enumerate((plane, line)[r])
        ]
        for copy in tops[g, r]:
            copy.start()

    def take_top(g, r):
        for copy in tops[g, r]:
            copy.wait_recv()
        best = amax[g]
        for i in range(3):
            best = jnp.maximum(best, top_rx[g, r, i].astype(F32))
        amax[g] = best

    def find_scales(g):
        top = amax[g]
        m = jnp.full((BLOCK, BLOCK), 2.0 ** (MBITS + 20), F32)
        f = jnp.full((BLOCK, BLOCK), 2.0**-20 / (2.0**MBITS * n), F32)
        for k in range(-20, 13):
            hit = top >= 2.0**k
            m = jnp.where(hit, 2.0 ** (MBITS - k - 1), m)
            f = jnp.where(hit, 2.0 ** (k + 1) / (2.0**MBITS * n), f)
        mult[g] = m.astype(BF16)
        factor[g] = f

    def spread(values, lane):
        pick = jnp.where(subs == lane, 1.0, 0.0).astype(BF16)
        return jnp.dot(values, pick, preferred_element_type=F32)

    def block_pair(g, b):
        c = at(b * BLOCK, BLOCK)
        for h in range(2):
            s = spread(mult[g], b + h * shift)
            a = own[h, :, :, :, :, c].reshape(BLOCK, BLOCK).astype(F32)
            p = peer[h, :, :, :, :, c].reshape(BLOCK, BLOCK).astype(F32)
            t = jnp.floor(a * s + 0.5) + jnp.floor(p * s + 0.5)
            pair[h, :, :, :, :, c] = t.astype(BF16).reshape(2, 2, 2, 16, BLOCK)

    early = 2

    def group(j):
        return 0 if j < early else 1

    started = {}

    def start(j, key, copies):
        for copy in copies:
            copy.start()
        started[j, key] = copies

    def arrived(j, key):
        for copy in started[j, key]:
            copy.wait_recv()

    def streams(j):
        size = WIDTHS[j] * BLOCK // 2
        start = first_block[j] * BLOCK
        return pl.ds(start, size), pl.ds(start + size, size)

    def send_pair(j):
        def body(b, _):
            block_pair(group(j), b)
            return 0

        lax.fori_loop(first_block[j], first_block[j + 1], body, 0, unroll=2)
        ca, cb = streams(j)
        start(
            j,
            "half",
            [
                remote(
                    pair.at[:, :, :, 1 - x, :, ca],
                    half_rx.at[:, :, :, :, ca],
                    half_send.at[j, 0],
                    half_recv.at[j, 0],
                    over_x,
                ),
                remote(
                    pair.at[:, :, 1 - y, :, :, cb],
                    half_rx.at[:, :, :, :, cb],
                    half_send.at[j, 1],
                    half_recv.at[j, 1],
                    over_y,
                ),
            ],
        )

    def send_half(j):
        arrived(j, "half")

        def first(b, _):
            c = at(b * BLOCK, BLOCK)
            near = pair[:, :, y, x, :, c].astype(F32) + half_rx[:, :, y, :, c].astype(F32)
            far = pair[:, :, 1 - y, x, :, c].astype(F32) + half_rx[:, :, 1 - y, :, c].astype(F32)
            quad[:, :, :, c] = near
            half_tx[:, :, :, c] = encode(far, 2)
            return 0

        def second(b, _):
            c = at(b * BLOCK, BLOCK)
            near = pair[:, :, y, x, :, c].astype(F32) + half_rx[:, :, x, :, c].astype(F32)
            far = pair[:, :, y, 1 - x, :, c].astype(F32) + half_rx[:, :, 1 - x, :, c].astype(F32)
            quad[:, :, :, c] = near
            half_tx[:, :, :, c] = encode(far, 2)
            return 0

        middle = first_block[j] + WIDTHS[j] // 2
        lax.fori_loop(first_block[j], middle, first, 0, unroll=2)
        lax.fori_loop(middle, first_block[j + 1], second, 0, unroll=2)
        start(
            j,
            "quad",
            [
                remote(
                    half_tx.at[:, :, :, c],
                    quad_rx.at[:, :, :, c],
                    quad_send.at[j, i],
                    quad_recv.at[j, i],
                    device,
                )
                for i, (c, device) in enumerate(zip(streams(j), (over_y, over_x)))
            ],
        )

    def send_quad(j):
        arrived(j, "quad")

        def body(b, _):
            c = at(b * BLOCK, BLOCK)
            total = quad[:, :, :, c] + decode(quad_rx[:, :, :, c].astype(F32), 2)
            quad[:, :, :, c] = total
            line_tx[:, :, :, c] = encode(total, 4)
            return 0

        lax.fori_loop(first_block[j], first_block[j + 1], body, 0, unroll=2)
        c = cols(j)
        start(
            j,
            "line",
            [
                remote(
                    line_tx.at[a, b, :, c],
                    line_rx.at[i, :, c],
                    line_send.at[j, i],
                    line_recv.at[j, i],
                    line[i],
                )
                for i, (a, b) in enumerate(line_spots)
            ],
        )

    def gather(j, i, spot, device):
        ref = gathered.at[spot]
        return remote(ref, ref, g_send.at[j, i], g_recv.at[j, i], device)

    def update(j):
        if j == 0:
            for near, far in states:
                near.wait()
                far.wait_recv()
        arrived(j, "line")
        rows = pl.ds(pl.multiple_of((chip % 8) * 16, 16), 16)
        scales = factor[group(j), rows, :]

        def body(b, _):
            c = at(b * BLOCK, BLOCK)
            lane = b + (chip // 8) * shift
            near = jnp.where(lanes[:16] == lane, scales, 0.0)
            s = jnp.sum(near, axis=1, keepdims=True)
            t = quad[z1, z0, :, c]
            for i in range(3):
                t = t + decode(line_rx[i, :, c].astype(F32), 4)
            g = (t * s).reshape(2, 8, BLOCK)
            new, m1, m2 = adam(g, state[0, :, :, c], state[1, :, :, c], state[2, :, :, c])
            fresh[0, :, :, c] = new
            fresh[1, :, :, c] = m1
            fresh[2, :, :, c] = m2
            fresh[3, :, :, c] = g
            v = new.reshape(16, BLOCK)
            w = jnp.max(jnp.abs(v), axis=1, keepdims=True) + 1e-06
            v = (v / w).astype(BF16).astype(F32) * w
            gathered[z1, z0, y, x, :, c] = v.astype(BF16)
            return 0

        lax.fori_loop(first_block[j], first_block[j + 1], body, 0, unroll=4)
        c = cols(j)
        c_out = cols_out(j)
        spot = (z1, z0, y, x, every, c)
        if j in LINE_LAST:
            start_plane(j, "g1", z1, z0)
        else:
            start_line(j, "g1", spot)
        start(
            j,
            "state",
            [
                remote(
                    fresh.at[:, 1 - core, :, c],
                    results.at[:, :, c_out],
                    out_send.at[j, 0],
                    out_recv.at[j, 0],
                    other_core,
                )
            ],
        )
        keep(fresh.at[:, core, :, c], results.at[:, :, c_out], out_sem.at[j, 0])

    kept = []

    def keep(src, dst, sem):
        kept.append(pltpu.make_async_copy(src, dst, sem))
        kept[-1].start()

    def start_line(j, key, spot):
        start(j, key, [gather(j, i, spot, device) for i, device in enumerate(line)])

    def start_plane(j, key, a, b):
        ca, cb = streams(j)
        start(
            j,
            key,
            [
                gather(j, 3, (a, b, y, x, every, ca), over_y),
                gather(j, 4, (a, b, y, x, every, cb), over_x),
            ],
        )

    def finish_plane(j, key, a, b):
        ca, cb = streams(j)
        start(
            j,
            key,
            [
                gather(j, 5, (a, b, every, x, every, ca), over_x),
                gather(j, 6, (a, b, y, every, every, cb), over_y),
            ],
        )

    def gather_first(j):
        arrived(j, "g1")
        if j in LINE_LAST:
            finish_plane(j, "g2", z1, z0)
        else:
            start_plane(j, "g2", every, every)

    def gather_second(j):
        arrived(j, "g2")
        if j in LINE_LAST:
            start_line(j, "g3", (z1, z0, every, every, every, cols(j)))
        else:
            finish_plane(j, "g3", every, every)

    def hand_out(j):
        arrived(j, "g3")
        src = gathered.at[:, :, :, :, :, cols(j)]
        dst = weights.at[:, :, :, :, :, cols_out(j)]
        start(j, "out", [remote(src, dst, out_send.at[j, 1], out_recv.at[j, 1], other_core)])
        keep(src, dst, out_sem.at[j, 1])

    find_max(0)
    send_top(0, 0)
    find_max(1)
    take_top(0, 0)
    send_top(0, 1)
    find_max(2)
    take_top(0, 1)
    find_scales(0)

    stages = (send_pair, send_half, send_quad, update, gather_first, gather_second, hand_out)
    for t in range(CHUNKS + len(stages) - 1):
        if t == early - 1:
            find_max(3)
            send_top(1, 0)
        if t == early:
            take_top(1, 1)
            find_scales(1)
        for s in range(len(stages)):
            if 0 <= t - s < CHUNKS:
                stages[s](t - s)
            if s == 0 and t == early - 1:
                take_top(1, 0)
                send_top(1, 1)
    for j in range(CHUNKS):
        arrived(j, "out")
        arrived(j, "state")
    for copy in kept:
        copy.wait()
    for swap in swaps:
        swap.wait_send()
    for copies in tops.values():
        for copy in copies:
            copy.wait_send()
    for _, far in states:
        far.wait_send()
    for copies in started.values():
        for copy in copies:
            copy.wait_send()


def hand_over(results, weights, master_new, one_new, two_new, grad, out, sem):
    copies = []
    for i in range(16):
        spot = (i // 8, i // 4 % 2, i // 2 % 2, i % 2)
        copies.append(pltpu.make_async_copy(weights.at[spot], out.at[spot], sem.at[i]))
    for i, ref in enumerate((master_new, one_new, two_new, grad)):
        copies.append(pltpu.make_async_copy(results.at[i], ref, sem.at[16 + i]))
    for copy in copies:
        copy.start()
    for copy in copies:
        copy.wait()


def fused(partials, master, moment_one, moment_two):
    n = lax.axis_size("dp")
    rows, full = partials.shape[1:]
    half = full // 2
    dims = (2, 2, 2, 2, 16)
    hbm = pl.BlockSpec(memory_space=pl.ANY)
    vmem = pl.BlockSpec(memory_space=pltpu.VMEM)
    slab = jax.ShapeDtypeStruct(dims + (full,), BF16)
    dma = pltpu.SemaphoreType.DMA
    results, weights = pl.pallas_call(
        functools.partial(kernel, n, half),
        out_shape=(pltpu.VMEM((4,) + master.shape, F32), pltpu.VMEM(dims + (full,), BF16)),
        in_specs=[hbm] * 4,
        out_specs=(hbm, hbm),
        scratch_shapes=[
            pltpu.VMEM(dims + (half,), BF16),
            pltpu.VMEM(dims + (half,), BF16),
            pltpu.VMEM(dims + (half,), BF16),
            pltpu.VMEM((2, BLOCK, BLOCK), F32),
            pltpu.VMEM((2, 2, BLOCK, BLOCK), BF16),
            pltpu.VMEM((2, 2, 3, BLOCK, BLOCK), BF16),
            pltpu.VMEM((2, BLOCK, BLOCK), BF16),
            pltpu.VMEM((2, BLOCK, BLOCK), F32),
            pltpu.VMEM((2, 2, 2, 16, half), BF16),
            pltpu.VMEM((2, 2, 16, half), BF16),
            pltpu.VMEM((2, 2, 16, half), BF16),
            pltpu.VMEM((2, 2, 16, half), F32),
            pltpu.VMEM((2, 2, 16, half), BF16),
            pltpu.VMEM((3, 16, half), BF16),
            pltpu.VMEM((3, 2, 8, half), F32),
            pltpu.VMEM((4, 2, 8, half), F32),
            pltpu.VMEM(dims + (half,), BF16),
            dma((SWAPS,)),
            dma((SWAPS,)),
            dma((SWAPS,)),
            dma((3,)),
            dma((3,)),
            dma((3,)),
            dma((2, 2, 3)),
            dma((2, 2, 3)),
            dma((CHUNKS, 2)),
            dma((CHUNKS, 2)),
            dma((CHUNKS, 2)),
            dma((CHUNKS, 2)),
            dma((CHUNKS, 3)),
            dma((CHUNKS, 3)),
            dma((CHUNKS, 7)),
            dma((CHUNKS, 7)),
            dma((CHUNKS, 2)),
            dma((CHUNKS, 2)),
            dma((CHUNKS, 2)),
        ],
        compiler_params=pltpu.CompilerParams(
            collective_id=0, has_side_effects=True, vmem_limit_bytes=52 * 2**20
        ),
        cost_estimate=pl.CostEstimate(
            flops=60 * rows * full, bytes_accessed=6 * rows * full, transcendentals=0
        ),
    )(partials.reshape(dims + (full,)), master, moment_one, moment_two)
    outs = pl.pallas_call(
        hand_over,
        out_shape=(jax.ShapeDtypeStruct(master.shape, F32),) * 4 + (slab,),
        in_specs=[vmem] * 2,
        out_specs=(hbm,) * 5,
        scratch_shapes=[
            dma((20,)),
        ],
        compiler_params=pltpu.CompilerParams(vmem_limit_bytes=8 * 2**20),
        cost_estimate=pl.CostEstimate(
            flops=0, bytes_accessed=5 * rows * full, transcendentals=0
        ),
    )(results, weights)
    return outs[:4] + (outs[4].reshape(rows, full),)


def block_scale(amax):
    powers = jnp.asarray([2.0**k for k in range(-20, 13)], jnp.float32)
    doubled = jnp.asarray([2.0 ** (k + 1) for k in range(-20, 13)], jnp.float32)
    inverse = jnp.asarray([2.0 ** (MBITS - k - 1) for k in range(-20, 13)], jnp.float32)
    hit = amax[..., None] >= powers
    scale = jnp.max(jnp.where(hit, doubled, jnp.float32(2.0 ** (-20))), axis=-1)
    mult = jnp.min(jnp.where(hit, inverse, jnp.float32(2.0 ** (MBITS + 20))), axis=-1)
    return (scale, mult)


def per_device(partials, master, moment_one, moment_two):
    devices = lax.axis_size("dp")
    local = partials[0]
    rows = local.shape[0]
    width = local.shape[1]
    nblk = width // BLOCK
    owned = master.shape[0]
    mags = jnp.abs(local.astype(jnp.float32)).reshape(rows, nblk, BLOCK)
    shared = lax.pmax(jnp.max(mags, axis=2).astype(jnp.bfloat16), "dp").astype(jnp.float32)
    scale_all, mult = block_scale(shared)
    vals = local.astype(jnp.float32).reshape(rows, nblk, BLOCK) * mult[:, :, None]
    mant = jnp.floor(vals + 0.5).reshape(rows, width)
    total = lax.psum_scatter(mant, "dp", scatter_dimension=0, tiled=True)
    start = lax.axis_index("dp") * owned
    scale = lax.dynamic_slice_in_dim(scale_all, start, owned, 0)
    total = total.reshape(owned, nblk, BLOCK)
    factor = scale / (2.0**MBITS * devices)
    reduced_grad = (total * factor[:, :, None]).reshape(owned, width)
    moment_one_new = 0.9 * moment_one + 0.1 * reduced_grad
    moment_two_new = 0.95 * moment_two + 0.05 * reduced_grad * reduced_grad
    first = moment_one_new / (1.0 - 0.9**STEP)
    second = moment_two_new / (1.0 - 0.95**STEP)
    update = first / (jnp.sqrt(second) + 1e-08)
    master_new = master - 0.001 * (update + 0.1 * master)
    blocks = master_new.reshape(owned, nblk, BLOCK)
    wscale = jnp.max(jnp.abs(blocks), axis=2) + 1e-06
    wmant = (blocks / wscale[:, :, None]).astype(jnp.bfloat16)
    own_weights = (
        (wmant.astype(jnp.float32) * wscale[:, :, None]).reshape(owned, width).astype(jnp.bfloat16)
    )
    weights = lax.all_gather(own_weights, "dp", axis=0, tiled=True)
    return (master_new, moment_one_new, moment_two_new, reduced_grad, weights)


def step_on_device(partials, master, moment_one, moment_two):
    if lax.axis_size("dp") == 32 and master.shape[0] == 8 and partials.shape[2] == 128 * BLOCK:
        return fused(partials, master, moment_one, moment_two)
    return per_device(partials, master, moment_one, moment_two)


def solution(mesh):
    in_specs = (P("dp", None, None), P("dp", None), P("dp", None), P("dp", None))
    out_specs = (P("dp", None), P("dp", None), P("dp", None), P("dp", None), P())
    return jax.shard_map(
        step_on_device, mesh=mesh, in_specs=in_specs, out_specs=out_specs, check_vma=False
    )
```
